128 devices in a mesh: frame: 32 (over z_lo, x, y), fsdp: 4 (over z_hi, core).
Axes of the slice: x: 4, y: 4, z: 4 (z_hi: 2, z_lo: 2; z = z_hi * 2 + z_lo), core: 2. Of those that a mesh axis runs over, the one named last changes fastest.
Arguments:
- frames_in: bfloat16 [8, 32, 256, 1024], P('fsdp', 'frame'), may hold values from -6 to 6
- sp_qkv: bfloat16 [1024, 3072], P('fsdp'), may hold values from -1 to 1
- sp_out: bfloat16 [1024, 1024], P('fsdp'), may hold values from -0.1875 to 0.1875
- tm_qkv: bfloat16 [1024, 3072], P('fsdp'), may hold values from -1 to 1
- tm_out: bfloat16 [1024, 1024], P('fsdp'), may hold values from -0.1875 to 0.1875
- cotangent: bfloat16 [8, 32, 256, 1024], P('fsdp', None, 'frame'), may hold values from -6 to 6
Outputs:
- block_out: bfloat16 [8, 32, 256, 1024], P('fsdp', None, 'frame')
- grad_in: float32 [8, 32, 256, 1024], P('fsdp', 'frame')
- grad_tm_qkv: float32 [1024, 3072], P('fsdp')
The draws below stay inside these ranges and needn't reach their ends.
All inputs are finite; a program needn't handle non-finite values.
Results may differ from the reference program's by a relative error of at most 0.035.
Values may be sent and summed in bfloat16 or wider, within the bound.
A program may use at most 192 MiB of HBM per device.

```python
import math
import jax
import jax.numpy as jnp
from jax import lax

D = 1024
HEADS = 8
S = 256
CLIPS = 8
FRAMES = 32


def packed_projection(key):
    first, second, third = jax.random.split(key, 3)
    base = 1.0 / math.sqrt(D)
    query = jax.random.truncated_normal(first, -4.0, 4.0, (D, D), jnp.float32) * base
    values = jax.random.truncated_normal(third, -4.0, 4.0, (D, D), jnp.float32) * base
    keys = jax.random.truncated_normal(second, -4.0, 4.0, (D, D), jnp.float32) * base
    return jnp.concatenate([query, keys, values], axis=1).astype(jnp.bfloat16)


def draw_sp_qkv(key, part):
    key = jax.random.fold_in(key, 11)
    return packed_projection(key)


def draw_tm_qkv(key, part):
    key = jax.random.fold_in(key, 12)
    return packed_projection(key)


def levels(rng, extent, cuts, low, largest):
    loudness = 1.0
    for dim, blocks in cuts:
        draws = jax.random.uniform(jax.random.fold_in(jax.random.fold_in(rng, 6), dim), (blocks,), jnp.float32, low / len(cuts), largest / len(cuts))
        loudness = loudness * jnp.repeat(jnp.exp(draws), extent[dim] // blocks).reshape((-1,) + (1,) * (len(extent) - 1 - dim))
    return loudness


def scatter_about(stream_key, dims, deviation, bound, shards=(), held_as=jnp.bfloat16):
    level = levels(stream_key, dims, shards, -0.22, 0.18) if shards else 1.0
    entries = jax.random.normal(stream_key, dims, jnp.float32) * deviation * level
    return jnp.minimum(jnp.maximum(entries, -bound), bound).astype(held_as)


def setup_inputs(seed: int = 0) -> dict:
    key_list = jax.random.split(jax.random.key(seed), 7)
    frames_in = scatter_about(key_list[0], (CLIPS, FRAMES, S, D), 1.0, 6.0, ((0, 4), (1, 32)))
    sp_qkv = draw_sp_qkv(jax.random.fold_in(key_list[6], 71), 0)
    sp_out = scatter_about(key_list[2], (D, D), D ** -0.5, 0.1875, ((0, 4),))
    tm_qkv = draw_tm_qkv(jax.random.fold_in(key_list[6], 71), 0)
    tm_out = scatter_about(key_list[4], (D, D), D ** -0.5, 0.1875, ((0, 4),))
    cotangent = scatter_about(key_list[5], (CLIPS, FRAMES, S, D), 1.0, 6.0, ((0, 4), (2, 32)))
    return {"frames_in": frames_in, "sp_qkv": sp_qkv, "sp_out": sp_out, "tm_qkv": tm_qkv, "tm_out": tm_out, "cotangent": cotangent}


EPS = 1e-05

def normalize(u):
    mean = lax.optimization_barrier(jnp.mean(u, axis=-1, keepdims=True))
    cent = u - mean
    rstd = lax.rsqrt(lax.optimization_barrier(jnp.mean(cent * cent, axis=-1, keepdims=True)) + EPS)
    return (cent * rstd, rstd)

def norm_back(normed, rstd, grad):
    first = lax.optimization_barrier(jnp.mean(grad, axis=-1, keepdims=True))
    second = lax.optimization_barrier(jnp.mean(grad * normed, axis=-1, keepdims=True))
    return rstd * (grad - first - normed * second)

def times(left, weight):
    flat = left.reshape(-1, left.shape[-1])
    prod = jnp.dot(flat, weight, preferred_element_type=jnp.float32)
    return prod.reshape(left.shape[:-1] + (weight.shape[1],))

def times_t(left, weight):
    flat = left.reshape(-1, left.shape[-1])
    prod = jnp.dot(flat, weight.T, preferred_element_type=jnp.float32)
    return prod.reshape(left.shape[:-1] + (weight.shape[0],))

def split_heads(packed, heads):
    width = packed.shape[-1] // 3
    shape = packed.shape[:-1] + (heads, width // heads)
    return [packed[..., i * width:(i + 1) * width].reshape(shape) for i in range(3)]

def attend(query, keys, values, causal):
    scale = query.shape[-1] ** (-0.5)
    scores = jnp.einsum('blxhe,bmxhe->bxhlm', query.astype(jnp.float32), keys.astype(jnp.float32)) * scale
    if causal:
        steps = scores.shape[-1]
        allowed = jnp.arange(steps)[:, None] >= jnp.arange(steps)[None, :]
        scores = jnp.where(allowed, scores, -jnp.inf)
    top = lax.optimization_barrier(jnp.max(scores, axis=-1, keepdims=True))
    expo = jnp.exp(scores - top)
    probs = expo / lax.optimization_barrier(jnp.sum(expo, axis=-1, keepdims=True))
    lowered = probs.astype(jnp.bfloat16)
    att = jnp.einsum('bxhlm,bmxhe->blxhe', lowered.astype(jnp.float32), values.astype(jnp.float32))
    return (att.astype(jnp.bfloat16), probs, lowered)

def attend_back(query, keys, values, probs, lowered, grad_att):
    scale = query.shape[-1] ** (-0.5)
    grad_f = grad_att.astype(jnp.float32)
    d_probs = jnp.einsum('blxhe,bmxhe->bxhlm', grad_f, values.astype(jnp.float32))
    d_values = jnp.einsum('bxhlm,blxhe->bmxhe', lowered.astype(jnp.float32), grad_f)
    d_scores = probs * (d_probs - lax.optimization_barrier(jnp.sum(d_probs * probs, axis=-1, keepdims=True))) * scale
    d_low = d_scores.astype(jnp.bfloat16).astype(jnp.float32)
    d_query = jnp.einsum('bxhlm,bmxhe->blxhe', d_low, keys.astype(jnp.float32))
    d_keys = jnp.einsum('bxhlm,blxhe->bmxhe', d_low, query.astype(jnp.float32))
    return (d_query, d_keys, d_values)

def join_heads(parts, shape):
    return jnp.concatenate([p.reshape(shape) for p in parts], axis=-1).astype(jnp.bfloat16)

def reference(frames_in, sp_qkv, sp_out, tm_qkv, tm_out, cotangent):

    def one_clip(total, pair):
        tokens, grad_out = pair
        frames, tokens_frame, width = tokens.shape
        normed_one, rstd_one = normalize(tokens.astype(jnp.float32))
        spatial_qkv = times(normed_one.astype(jnp.bfloat16), sp_qkv).astype(jnp.bfloat16)
        sq, sk, sv = split_heads(spatial_qkv.reshape(frames, tokens_frame, 1, 3 * width), HEADS)
        spatial_att, sp_probs, sp_low = attend(sq, sk, sv, False)
        spatial_att = spatial_att.reshape(frames, tokens_frame, width)
        stream = (tokens.astype(jnp.float32) + times(spatial_att, sp_out)).astype(jnp.bfloat16)
        stream = lax.optimization_barrier(stream)
        normed_two, rstd_two = normalize(stream.astype(jnp.float32))
        low_two = normed_two.astype(jnp.bfloat16)
        temporal_qkv = times(low_two, tm_qkv).astype(jnp.bfloat16)
        tq, tk, tv = split_heads(temporal_qkv.reshape(1, frames, tokens_frame, 3 * width), HEADS)
        temporal_att, tm_probs, tm_low = attend(tq, tk, tv, True)
        temporal_att = temporal_att.reshape(frames, tokens_frame, width)
        block_out = (stream.astype(jnp.float32) + times(temporal_att, tm_out)).astype(jnp.bfloat16)
        d_temporal_att = times_t(grad_out, tm_out).astype(jnp.bfloat16)
        d_att_heads = d_temporal_att.reshape(tq.shape)
        parts = attend_back(tq, tk, tv, tm_probs, tm_low, d_att_heads)
        d_temporal_qkv = join_heads(parts, (frames, tokens_frame, width))
        grad_w = jnp.dot(low_two.reshape(-1, width).T, d_temporal_qkv.reshape(-1, 3 * width), preferred_element_type=jnp.float32)
        d_stream = grad_out.astype(jnp.float32) + norm_back(normed_two, rstd_two, times_t(d_temporal_qkv, tm_qkv))
        d_spatial_att = times_t(d_stream.astype(jnp.bfloat16), sp_out).astype(jnp.bfloat16)
        parts = attend_back(sq, sk, sv, sp_probs, sp_low, d_spatial_att.reshape(sq.shape))
        d_spatial_qkv = join_heads(parts, (frames, tokens_frame, width))
        grad_in = d_stream + norm_back(normed_one, rstd_one, times_t(d_spatial_qkv, sp_qkv))
        return (total + grad_w, (block_out, grad_in))
    start = jnp.zeros((sp_qkv.shape[0], sp_qkv.shape[1]), jnp.float32)
    total, (block_out, grad_in) = lax.scan(one_clip, start, (frames_in, cotangent))
    return (block_out, grad_in, total)
```

```python
import jax
import jax.numpy as jnp
from jax import lax
from jax.sharding import PartitionSpec as P

HEADS = 8


EPS = 1e-05


def normalize(u):
    mean = jnp.mean(u, axis=-1, keepdims=True)
    cent = u - mean
    rstd = lax.rsqrt(jnp.mean(cent * cent, axis=-1, keepdims=True) + EPS)
    return (cent * rstd, rstd)


def norm_back(normed, rstd, grad):
    first = jnp.mean(grad, axis=-1, keepdims=True)
    second = jnp.mean(grad * normed, axis=-1, keepdims=True)
    return rstd * (grad - first - normed * second)


def times(left, weight):
    flat = left.reshape(-1, left.shape[-1])
    prod = jnp.dot(flat, weight, preferred_element_type=jnp.float32)
    return prod.reshape(left.shape[:-1] + (weight.shape[1],))


def times_t(left, weight):
    flat = left.reshape(-1, left.shape[-1])
    prod = lax.dot_general(
        flat, weight, (((1,), (1,)), ((), ())), preferred_element_type=jnp.float32
    )
    return prod.reshape(left.shape[:-1] + (weight.shape[0],))


def split_heads(packed, heads):
    width = packed.shape[-1] // 3
    shape = packed.shape[:-1] + (heads, width // heads)
    return [packed[..., i * width : (i + 1) * width].reshape(shape) for i in range(3)]


def attend(query, keys, values, causal):
    scale = query.shape[-1] ** (-0.5)
    scores = (
        jnp.einsum("blxhe,bmxhe->bxhlm", query, keys, preferred_element_type=jnp.float32) * scale
    )
    if causal:
        steps = scores.shape[-1]
        allowed = jnp.arange(steps)[:, None] >= jnp.arange(steps)[None, :]
        scores = jnp.where(allowed, scores, -jnp.inf)
    top = jnp.max(scores, axis=-1, keepdims=True)
    expo = jnp.exp(scores - top)
    probs = expo / jnp.sum(expo, axis=-1, keepdims=True)
    lowered = probs.astype(jnp.bfloat16)
    att = jnp.einsum("bxhlm,bmxhe->blxhe", lowered, values, preferred_element_type=jnp.float32)
    return (att.astype(jnp.bfloat16), probs, lowered)


def attend_back(query, keys, values, probs, lowered, grad_att):
    scale = query.shape[-1] ** (-0.5)
    d_probs = jnp.einsum("blxhe,bmxhe->bxhlm", grad_att, values, preferred_element_type=jnp.float32)
    d_values = jnp.einsum(
        "bxhlm,blxhe->bmxhe", lowered, grad_att, preferred_element_type=jnp.float32
    )
    d_scores = probs * (d_probs - jnp.sum(d_probs * probs, axis=-1, keepdims=True)) * scale
    d_low = d_scores.astype(jnp.bfloat16)
    d_query = jnp.einsum("bxhlm,bmxhe->blxhe", d_low, keys, preferred_element_type=jnp.float32)
    d_keys = jnp.einsum("bxhlm,blxhe->bmxhe", d_low, query, preferred_element_type=jnp.float32)
    return (d_query, d_keys, d_values)


def join_heads(parts, shape):
    return jnp.concatenate([p.reshape(shape) for p in parts], axis=-1).astype(jnp.bfloat16)


def gather_rows(shard):
    rows = shard.shape[0] // lax.axis_size("frame")
    mine = lax.dynamic_slice_in_dim(shard, lax.axis_index("frame") * rows, rows, 0)
    return lax.all_gather(mine, ("fsdp", "frame"), axis=0, tiled=True)


def body(frames_in, sp_qkv, sp_out, tm_qkv, tm_out, cotangent):
    clips, frames_local, tokens_frame, width = frames_in.shape
    sp_qkv_all, sp_out_all = (gather_rows(sp_qkv), gather_rows(sp_out))
    tm_qkv_all, tm_out_all = (gather_rows(tm_qkv), gather_rows(tm_out))
    normed_one, rstd_one = normalize(frames_in.astype(jnp.float32))
    spatial_qkv = times(normed_one.astype(jnp.bfloat16), sp_qkv_all).astype(jnp.bfloat16)
    sq, sk, sv = split_heads(
        spatial_qkv.reshape(clips * frames_local, tokens_frame, 1, 3 * width), HEADS
    )
    spatial_att, sp_probs, sp_low = attend(sq, sk, sv, False)
    spatial_att = spatial_att.reshape(frames_in.shape)
    stream = (frames_in.astype(jnp.float32) + times(spatial_att, sp_out_all)).astype(jnp.bfloat16)
    stream_pos = lax.all_to_all(stream, "frame", split_axis=2, concat_axis=1, tiled=True)
    normed_two, rstd_two = normalize(stream_pos.astype(jnp.float32))
    low_two = normed_two.astype(jnp.bfloat16)
    qkv_pos = times(low_two, tm_qkv_all).astype(jnp.bfloat16)
    tq, tk, tv = split_heads(qkv_pos, HEADS)
    temporal_att, tm_probs, tm_low = attend(tq, tk, tv, True)
    temporal_att = temporal_att.reshape(stream_pos.shape)
    block_out = (stream_pos.astype(jnp.float32) + times(temporal_att, tm_out_all)).astype(
        jnp.bfloat16
    )
    d_temporal_att = times_t(cotangent, tm_out_all).astype(jnp.bfloat16)
    parts = attend_back(tq, tk, tv, tm_probs, tm_low, d_temporal_att.reshape(tq.shape))
    d_qkv_pos = join_heads(parts, stream_pos.shape)
    d_stream_pos = cotangent.astype(jnp.float32) + norm_back(
        normed_two, rstd_two, times_t(d_qkv_pos, tm_qkv_all)
    )
    d_stream_low = lax.all_to_all(
        d_stream_pos.astype(jnp.bfloat16), "frame", split_axis=1, concat_axis=2, tiled=True
    )
    d_stream = d_stream_low.astype(jnp.float32)
    left_rows = low_two.reshape(-1, width)
    right_rows = d_qkv_pos.reshape(-1, 3 * width)
    piece = lax.psum_scatter(
        lax.dot_general(
            left_rows, right_rows, (((0,), (0,)), ((), ())), preferred_element_type=jnp.float32
        ).astype(jnp.bfloat16),
        ("fsdp", "frame"),
        scatter_dimension=0,
        tiled=True,
    )
    grad_tm_qkv = lax.all_gather(piece, "frame", axis=0, tiled=True).astype(jnp.float32)
    d_spatial_att = times_t(d_stream_low, sp_out_all).astype(jnp.bfloat16)
    parts = attend_back(sq, sk, sv, sp_probs, sp_low, d_spatial_att.reshape(sq.shape))
    d_spatial_qkv = join_heads(parts, frames_in.shape)
    grad_in = d_stream + norm_back(normed_one, rstd_one, times_t(d_spatial_qkv, sp_qkv_all))
    return (block_out, grad_in, grad_tm_qkv)


def solution(mesh):
    in_specs = (
        P("fsdp", "frame", None, None),
        P("fsdp", None),
        P("fsdp", None),
        P("fsdp", None),
        P("fsdp", None),
        P("fsdp", None, "frame", None),
    )
    out_specs = (P("fsdp", None, "frame", None), P("fsdp", "frame", None, None), P("fsdp", None))
    return jax.shard_map(body, mesh=mesh, in_specs=in_specs, out_specs=out_specs, check_vma=False)
```

```python
import functools

import jax
import jax.numpy as jnp
from jax import lax
from jax.experimental import pallas as pl
from jax.experimental.pallas import tpu as pltpu
from jax.sharding import PartitionSpec as P

MESH = pl.DeviceIdType.MESH
F32 = jnp.float32
BF16 = jnp.bfloat16
EPS = 1e-05
HEADS = 8
HEAD = 128
SCALE = HEAD**-0.5
D = 1024
T = 512
CLIP = 256
VMEM_LIMIT = 60 * 1024 * 1024


def dot(left, right):
    return lax.dot_general(left, right, (((1,), (0,)), ((), ())), preferred_element_type=F32)


def dot_nt(left, right):
    return lax.dot_general(left, right, (((1,), (1,)), ((), ())), preferred_element_type=F32)


def dot_tn(left, right):
    return lax.dot_general(left, right, (((0,), (0,)), ((), ())), preferred_element_type=F32)


def ds(index, size):
    return pl.ds(pl.multiple_of(index * size, size), size)


def loop(count, unroll=1):
    def run(body):
        def step(i, carry):
            body(i)
            return carry

        lax.fori_loop(0, count, step, 0, unroll=unroll)

    return run


def normalize(u):
    mean = jnp.mean(u, axis=-1, keepdims=True)
    cent = u - mean
    rstd = lax.rsqrt(jnp.mean(cent * cent, axis=-1, keepdims=True) + EPS)
    return cent * rstd, rstd


def norm_back(normed, rstd, grad):
    first = jnp.mean(grad, axis=-1, keepdims=True)
    second = jnp.mean(grad * normed, axis=-1, keepdims=True)
    return rstd * (grad - first - normed * second)


def softmax(scores):
    top = jnp.max(scores, axis=-1, keepdims=True)
    expo = jnp.exp(scores - top)
    return expo / jnp.sum(expo, axis=-1, keepdims=True)


def attend_back(q, k, v, probs, low, a):
    d_probs = dot_nt(a, v)
    d_v = dot_tn(low, a)
    prod = d_probs * probs
    d_s = ((prod - probs * jnp.sum(prod, axis=-1, keepdims=True)) * SCALE).astype(BF16)
    return dot(d_s, k), dot_tn(d_s, q), d_v


def part(i, head):
    return pl.ds(pl.multiple_of((i * HEADS + head) * HEAD, HEAD), HEAD)


def to_chunks(rows):
    parts = []
    for d in range(32):
        parts.append(rows[8 * d : 8 * d + 8])
        parts.append(rows[CLIP + 8 * d : CLIP + 8 * d + 8])
    return jnp.concatenate(parts, axis=0)


def from_chunks(rows):
    return jnp.concatenate(
        [rows[16 * d + 8 * c : 16 * d + 8 * c + 8] for c in range(2) for d in range(32)], axis=0
    )


def spatial_kernel(x_ref, wqkv_ref, wo_ref, qkv_ref, stream_ref, nrm, att):
    @loop(8)
    def _(r):
        rows = ds(r, 64)
        nrm[rows, :] = normalize(x_ref[rows, :].astype(F32))[0].astype(BF16)

    @loop(6)
    def _(n):
        cols = ds(n, 512)
        qkv_ref[:, cols] = dot(nrm[...], wqkv_ref[:, cols]).astype(BF16)

    @loop(8)
    def _(h):
        for c in range(2):
            rows = pl.ds(c * CLIP, CLIP)
            q, k, v = (qkv_ref[rows, part(i, h)] for i in range(3))
            low = softmax(dot_nt(q, k) * SCALE).astype(BF16)
            att[rows, part(0, h)] = dot(low, v).astype(BF16)

    @loop(4)
    def _(n):
        cols = ds(n, 256)
        out = dot(att[...], wo_ref[:, cols]) + x_ref[:, cols].astype(F32)
        stream_ref[:, cols] = to_chunks(out).astype(BF16)


def temporal_kernel(
    s_ref, cot_ref, wqkv_ref, wo_ref, out_ref, dchunk_ref, low_ref, dqkv_ref,
    stream, qkv, da, att, bias, grad,
):
    @loop(8)
    def _(n):
        cols = ds(n, 128)
        stream[:, cols] = from_chunks(s_ref[:, cols].astype(F32)).astype(BF16)

    @loop(8)
    def _(r):
        rows = ds(r, 64)
        low_ref[rows, :] = normalize(stream[rows, :].astype(F32))[0].astype(BF16)

    @loop(6)
    def _(n):
        cols = ds(n, 512)
        qkv[:, cols] = dot(low_ref[...], wqkv_ref[:, cols]).astype(BF16)

    @loop(2)
    def _(n):
        cols = ds(n, 512)
        da[:, cols] = dot_nt(cot_ref[...], wo_ref[cols, :]).astype(BF16)

    row = lax.broadcasted_iota(jnp.int32, (CLIP, CLIP), 0)
    col = lax.broadcasted_iota(jnp.int32, (CLIP, CLIP), 1)
    allowed = (col <= row) & (((row - col) & 7) == 0)
    bias[...] = jnp.where(allowed, 0.0, -1e30)

    @loop(8)
    def _(h):
        for c in range(2):
            rows = pl.ds(c * CLIP, CLIP)
            q, k, v = (qkv[rows, part(i, h)] for i in range(3))
            probs = softmax(dot_nt(q, k) * SCALE + bias[...])
            low = probs.astype(BF16)
            att[rows, part(0, h)] = dot(low, v).astype(BF16)
            parts = attend_back(q, k, v, probs, low, da[rows, part(0, h)])
            for i in range(3):
                dqkv_ref[rows, part(i, h)] = parts[i].astype(BF16)

    @loop(2)
    def _(n):
        cols = ds(n, 512)
        out = dot(att[...], wo_ref[:, cols]) + stream[:, cols].astype(F32)
        out_ref[:, cols] = out.astype(BF16)

    @loop(4)
    def _(n):
        cols = ds(n, 256)
        grad[:, cols] = dot_nt(dqkv_ref[...], wqkv_ref[cols, :])

    @loop(8)
    def _(r):
        rows = ds(r, 64)
        normed, rstd = normalize(stream[rows, :].astype(F32))
        grad[rows, :] = cot_ref[rows, :].astype(F32) + norm_back(normed, rstd, grad[rows, :])

    @loop(8)
    def _(n):
        cols = ds(n, 128)
        dchunk_ref[:, cols] = to_chunks(grad[:, cols]).astype(BF16)


def spatial_back_kernel(x_ref, d_ref, qkv_ref, wqkv_ref, wo_ref, out_ref, dstr, da, dqkv):
    @loop(8)
    def _(n):
        cols = ds(n, 128)
        dstr[:, cols] = from_chunks(d_ref[:, cols].astype(F32)).astype(BF16)

    @loop(2)
    def _(n):
        cols = ds(n, 512)
        da[:, cols] = dot_nt(dstr[...], wo_ref[cols, :]).astype(BF16)

    @loop(8)
    def _(h):
        for c in range(2):
            rows = pl.ds(c * CLIP, CLIP)
            q, k, v = (qkv_ref[rows, part(i, h)] for i in range(3))
            probs = softmax(dot_nt(q, k) * SCALE)
            parts = attend_back(q, k, v, probs, probs.astype(BF16), da[rows, part(0, h)])
            for i in range(3):
                dqkv[rows, part(i, h)] = parts[i].astype(BF16)

    @loop(4)
    def _(n):
        cols = ds(n, 256)
        out_ref[:, cols] = dot_nt(dqkv[...], wqkv_ref[cols, :])

    @loop(8)
    def _(r):
        rows = ds(r, 64)
        normed, rstd = normalize(x_ref[rows, :].astype(F32))
        out_ref[rows, :] = dstr[rows, :].astype(F32) + norm_back(normed, rstd, out_ref[rows, :])


class Place:
    def __init__(self):
        frame, fsdp = lax.axis_index("frame"), lax.axis_index("fsdp")
        self.lo, x, y = lax.div(frame, 16), lax.rem(lax.div(frame, 4), 4), lax.rem(frame, 4)
        self.hi, self.core = lax.div(fsdp, 2), lax.rem(fsdp, 2)
        self.x, self.y = x, y
        self.a = x + self.core * (y - x)
        self.b = y + self.core * (x - y)
        self.ap, self.am = lax.rem(self.a + 1, 4), lax.rem(self.a + 3, 4)
        self.bp, self.bm = lax.rem(self.b + 1, 4), lax.rem(self.b + 3, 4)
        self.a2, self.b2 = lax.rem(self.a + 2, 4), lax.rem(self.b + 2, 4)
        self.fsdp = fsdp
        self.sibling = (frame, self.hi * 2 + 1 - self.core)
        self.cross = ((1 - self.lo) * 16 + x * 4 + y, (1 - self.hi) * 2 + self.core)
        self.twin = ((1 - self.lo) * 16 + x * 4 + y, fsdp)
        self.a_next, self.a_prev = self.at(self.ap, self.b), self.at(self.am, self.b)
        self.b_next, self.b_prev = self.at(self.a, self.bp), self.at(self.a, self.bm)

    def at(self, a, b):
        x = a + self.core * (b - a)
        y = b + self.core * (a - b)
        return (self.lo * 16 + x * 4 + y, self.fsdp)


def greet(devices):
    barrier = pltpu.get_barrier_semaphore()
    for device in devices:
        pl.semaphore_signal(barrier, inc=1, device_id=device, device_id_type=MESH)
    pl.semaphore_wait(barrier, len(devices))


class Copies:
    def __init__(self, send, recv):
        self.send, self.recv, self.count, self.started = send, recv, 0, []

    def start(self, src, dst, device):
        i = self.count
        self.count += 1
        copy = pltpu.make_async_remote_copy(
            src_ref=src, dst_ref=dst, send_sem=self.send.at[i], recv_sem=self.recv.at[i],
            device_id=device, device_id_type=MESH,
        )
        copy.start()
        self.started.append(copy)
        return copy

    def finish(self):
        for copy in self.started:
            copy.wait_send()


def rows_at(index, size):
    return pl.ds(pl.multiple_of(index, size), size)


def gather_steps(copies, here, shard, out):
    width = shard.shape[1]
    half = width // 2
    lo, hi = pl.ds(0, half), pl.ds(half, half)
    own = here.fsdp * 256
    base = ((1 - here.hi) * 2 + here.core) * 256

    piece = (here.b * 4 + here.a) * 16
    cross = copies.start(shard.at[rows_at(piece, 16), :], out.at[rows_at(own + piece, 16), :], here.cross)
    mine = copies.start(shard, out.at[rows_at(own, 256), :], here.sibling)
    yield
    cross.wait_recv()

    def spread(size, offset, here_at, before, after, nxt, prv):
        def rows(i):
            return rows_at(base + offset + i * size, size)

        block = out.at[rows(here_at), :]
        right = copies.start(block, block, nxt)
        left = copies.start(block, block, prv)
        yield
        right.wait_recv()
        ahead = out.at[rows(before), lo]
        right2 = copies.start(ahead, ahead, nxt)
        left.wait_recv()
        ahead = out.at[rows(after), hi]
        left2 = copies.start(ahead, ahead, prv)
        yield
        right2.wait_recv()
        left2.wait_recv()

    yield from spread(16, here.b * 64, here.a, here.am, here.ap, here.a_next, here.a_prev)

    def over(i):
        block = out.at[rows_at(base + i * 64, 64), :]
        return copies.start(block, block, here.sibling)

    spreading = spread(64, 0, here.b, here.bm, here.bp, here.b_next, here.b_prev)
    next(spreading)
    last = [over(here.b)]
    yield
    next(spreading)
    last += [over(here.bm), over(here.bp)]
    yield
    for _ in spreading:
        pass
    last.append(over(here.b2))
    yield
    mine.wait_recv()
    for copy in last:
        copy.wait_recv()


GATHER_COPIES = 14


def gather_kernel(*refs):
    shards, outs, (send, recv, local) = refs[:4], refs[4:8], refs[8:]
    here = Place()
    greet([here.sibling, here.cross, here.a_next, here.a_prev, here.b_next, here.b_prev])
    copies = Copies(send, recv)
    locals_ = []
    for i in range(4):
        copy = pltpu.make_async_copy(
            shards[i], outs[i].at[rows_at(here.fsdp * 256, 256), :], local.at[i]
        )
        locals_.append(copy)
    waiting = [gather_steps(copies, here, shards[i], outs[i]) for i in range(4)]
    for steps in waiting:
        next(steps)
    for copy in locals_:
        copy.start()
    while waiting:
        for steps in list(waiting):
            try:
                next(steps)
            except StopIteration:
                waiting.remove(steps)
    copies.finish()
    for copy in locals_:
        copy.wait()


def reduce_kernel(low_ref, dq_ref, out_ref, give, take, held, rb1, rb2, ra1, ra2, piece, rz, total, send, recv):
    here = Place()
    greet([here.sibling, here.cross, here.twin, here.a_next, here.a_prev, here.b_next, here.b_prev])
    copies = Copies(send, recv)
    half = 3 * D // 2
    lo, hi = pl.ds(0, half), pl.ds(half, half)

    def left(h, core):
        return low_ref[:, rows_at((h * 2 + core) * 256, 256)]

    siblings = []
    for h in range(2):

        @loop(6)
        def _(n):
            cols = ds(n, 512)
            give[h, :, cols] = dot_tn(left(h, 1 - here.core), dq_ref[:, cols]).astype(BF16)

        siblings.append(copies.start(give.at[h], take.at[h], here.sibling))
    for h in range(2):
        siblings[h].wait_recv()

        @loop(6)
        def _(n):
            cols = ds(n, 512)
            held[h, :, cols] = (
                dot_tn(left(h, here.core), dq_ref[:, cols]) + take[h, :, cols].astype(F32)
            ).astype(BF16)

    def add(rows, cols, *others):
        total_ = held[:, rows, cols].astype(F32)
        for other in others:
            total_ = total_ + other.astype(F32)
        held[:, rows, cols] = total_.astype(BF16)

    def scatter(size, offset, at, before, after, opposite, nxt, prv, first, second):
        def rows(i):
            return rows_at(offset + i * size, size)

        def send_(i, cols, dst, device):
            return copies.start(held.at[:, rows(i), cols], dst, device)

        one = send_(opposite, lo, first.at[:, :, lo], nxt)
        two = send_(opposite, hi, first.at[:, :, hi], prv)
        three = send_(after, hi, second.at[0, :, :, hi], nxt)
        four = send_(before, lo, second.at[1, :, :, lo], prv)
        one.wait_recv()
        add(rows(after), lo, first[:, :, lo])
        five = send_(after, lo, second.at[0, :, :, lo], nxt)
        two.wait_recv()
        add(rows(before), hi, first[:, :, hi])
        six = send_(before, hi, second.at[1, :, :, hi], prv)
        for copy in (three, four, five, six):
            copy.wait_recv()
        add(rows(at), slice(None), second[0], second[1])

    scatter(64, 0, here.b, here.bm, here.bp, here.b2, here.b_next, here.b_prev, rb1, rb2)
    base = here.b * 64
    scatter(16, base, here.a, here.am, here.ap, here.a2, here.a_next, here.a_prev, ra1, ra2)

    mine = rows_at(base + here.a * 16, 16)
    cross = copies.start(held.at[1 - here.hi, mine, :], rz.at[0], here.cross)
    cross.wait_recv()
    piece[...] = (held[here.hi, mine, :].astype(F32) + rz[0].astype(F32)).astype(BF16)
    twin = copies.start(piece, rz.at[1], here.twin)
    twin.wait_recv()
    total[mine, :] = (piece[...].astype(F32) + rz[1].astype(F32)).astype(BF16)

    def spread(size, offset, at, before, after, nxt, prv):
        def rows(i):
            return rows_at(offset + i * size, size)

        block = total.at[rows(at), :]
        right = copies.start(block, block, nxt)
        left_ = copies.start(block, block, prv)
        right.wait_recv()
        ahead = total.at[rows(before), lo]
        right2 = copies.start(ahead, ahead, nxt)
        left_.wait_recv()
        ahead = total.at[rows(after), hi]
        left2 = copies.start(ahead, ahead, prv)
        right2.wait_recv()
        left2.wait_recv()

    spread(16, base, here.a, here.am, here.ap, here.a_next, here.a_prev)
    spread(64, 0, here.b, here.bm, here.bp, here.b_next, here.b_prev)
    out_ref[...] = total[...].astype(F32)
    copies.finish()


REDUCE_COPIES = 24
VM = pl.BlockSpec(memory_space=pltpu.VMEM)
ANY = pl.BlockSpec(memory_space=pl.ANY)


def sds(shape, dtype):
    return jax.ShapeDtypeStruct(shape, dtype)


def call(kernel, ins, outs, scratch, collective=None, specs=None, out_specs=None):
    extra = {} if collective is None else dict(collective_id=collective, has_side_effects=True)
    return pl.pallas_call(
        kernel,
        out_shape=outs,
        in_specs=specs or [VM] * len(ins),
        out_specs=out_specs or [VM] * len(outs),
        scratch_shapes=scratch,
        compiler_params=pltpu.CompilerParams(vmem_limit_bytes=VMEM_LIMIT, **extra),
    )(*ins)


def body(frames_in, sp_qkv, sp_out, tm_qkv, tm_out, cotangent):
    x = frames_in.reshape(T, D)
    cot = cotangent.reshape(T, D)
    shards = (sp_qkv, sp_out, tm_qkv, tm_out)
    dma = pltpu.SemaphoreType.DMA
    sp_qkv, sp_out, tm_qkv, tm_out = call(
        gather_kernel, shards, [sds((D, w.shape[1]), BF16) for w in shards],
        [dma((4 * GATHER_COPIES,)), dma((4 * GATHER_COPIES,)), dma((4,))],
        collective=0, specs=[ANY] * 4, out_specs=[ANY] * 4,
    )
    qkv, chunks = call(
        spatial_kernel, (x, sp_qkv, sp_out), [sds((T, 3 * D), BF16), sds((T, D), BF16)],
        [pltpu.VMEM((T, D), BF16), pltpu.VMEM((T, D), BF16)],
    )

    def exchange(rows):
        return lax.all_to_all(
            rows.reshape(32, 16, D), "frame", split_axis=0, concat_axis=0, tiled=True
        ).reshape(T, D)

    block_out, d_chunks, low, d_qkv = call(
        temporal_kernel, (exchange(chunks), cot, tm_qkv, tm_out),
        [sds((T, D), BF16), sds((T, D), BF16), sds((T, D), BF16), sds((T, 3 * D), BF16)],
        [
            pltpu.VMEM((T, D), BF16), pltpu.VMEM((T, 3 * D), BF16), pltpu.VMEM((T, D), BF16),
            pltpu.VMEM((T, D), BF16), pltpu.VMEM((CLIP, CLIP), F32), pltpu.VMEM((T, D), F32),
        ],
    )
    (grad_tm,) = call(
        reduce_kernel, (low, d_qkv), [sds((256, 3 * D), F32)],
        [
            pltpu.VMEM((2, 256, 3 * D), BF16), pltpu.VMEM((2, 256, 3 * D), BF16),
            pltpu.VMEM((2, 256, 3 * D), BF16),
            pltpu.VMEM((2, 64, 3 * D), BF16), pltpu.VMEM((2, 2, 64, 3 * D), BF16),
            pltpu.VMEM((2, 16, 3 * D), BF16), pltpu.VMEM((2, 2, 16, 3 * D), BF16),
            pltpu.VMEM((16, 3 * D), BF16), pltpu.VMEM((2, 16, 3 * D), BF16),
            pltpu.VMEM((256, 3 * D), BF16),
            dma((REDUCE_COPIES,)), dma((REDUCE_COPIES,)),
        ],
        collective=1,
    )
    (grad_in,) = call(
        spatial_back_kernel, (x, exchange(d_chunks), qkv, sp_qkv, sp_out), [sds((T, D), F32)],
        [pltpu.VMEM((T, D), BF16), pltpu.VMEM((T, D), BF16), pltpu.VMEM((T, 3 * D), BF16)],
    )
    return (block_out.reshape(cotangent.shape), grad_in.reshape(frames_in.shape), grad_tm)


def solution(mesh):
    in_specs = (
        P("fsdp", "frame", None, None),
        P("fsdp", None),
        P("fsdp", None),
        P("fsdp", None),
        P("fsdp", None),
        P("fsdp", None, "frame", None),
    )
    out_specs = (P("fsdp", None, "frame", None), P("fsdp", "frame", None, None), P("fsdp", None))
    return jax.shard_map(body, mesh=mesh, in_specs=in_specs, out_specs=out_specs, check_vma=False)
```

```python
import functools

import jax
import jax.numpy as jnp
from jax import lax
from jax.experimental import pallas as pl
from jax.experimental.pallas import tpu as pltpu
from jax.sharding import PartitionSpec as P

MESH = pl.DeviceIdType.MESH
F32 = jnp.float32
BF16 = jnp.bfloat16
EPS = 1e-05
HEADS = 8
HEAD = 128
SCALE = HEAD**-0.5
D = 1024
T = 512
CLIP = 256
VMEM_LIMIT = 60 * 1024 * 1024


def dot(left, right):
    return lax.dot_general(left, right, (((1,), (0,)), ((), ())), preferred_element_type=F32)


def dot_nt(left, right):
    return lax.dot_general(left, right, (((1,), (1,)), ((), ())), preferred_element_type=F32)


def dot_tn(left, right):
    return lax.dot_general(left, right, (((0,), (0,)), ((), ())), preferred_element_type=F32)


def ds(index, size):
    return pl.ds(pl.multiple_of(index * size, size), size)


def loop(count, unroll=1):
    def run(body):
        def step(i, carry):
            body(i)
            return carry

        lax.fori_loop(0, count, step, 0, unroll=unroll)

    return run


def normalize(u):
    mean = jnp.mean(u, axis=-1, keepdims=True)
    cent = u - mean
    rstd = lax.rsqrt(jnp.mean(cent * cent, axis=-1, keepdims=True) + EPS)
    return cent * rstd, rstd


def norm_back(normed, rstd, grad):
    first = jnp.mean(grad, axis=-1, keepdims=True)
    second = jnp.mean(grad * normed, axis=-1, keepdims=True)
    return rstd * (grad - first - normed * second)


def softmax(scores):
    top = jnp.max(scores, axis=-1, keepdims=True)
    expo = jnp.exp(scores - top)
    return expo / jnp.sum(expo, axis=-1, keepdims=True)


def attend_back(q, k, v, probs, low, a):
    d_probs = dot_nt(a, v)
    d_v = dot_tn(low, a)
    prod = d_probs * probs
    d_s = ((prod - probs * jnp.sum(prod, axis=-1, keepdims=True)) * SCALE).astype(BF16)
    return dot(d_s, k), dot_tn(d_s, q), d_v


def part(i, head):
    return pl.ds(pl.multiple_of((i * HEADS + head) * HEAD, HEAD), HEAD)


def rows_at(index, size):
    return pl.ds(pl.multiple_of(index, size), size)


class Place:
    def __init__(self):
        frame, fsdp = lax.axis_index("frame"), lax.axis_index("fsdp")
        self.lo, x, y = lax.div(frame, 16), lax.rem(lax.div(frame, 4), 4), lax.rem(frame, 4)
        self.hi, self.core = lax.div(fsdp, 2), lax.rem(fsdp, 2)
        self.x, self.y = x, y
        self.a = x + self.core * (y - x)
        self.b = y + self.core * (x - y)
        self.ap, self.am = lax.rem(self.a + 1, 4), lax.rem(self.a + 3, 4)
        self.bp, self.bm = lax.rem(self.b + 1, 4), lax.rem(self.b + 3, 4)
        self.a2, self.b2 = lax.rem(self.a + 2, 4), lax.rem(self.b + 2, 4)
        self.fsdp, self.frame = fsdp, frame
        self.far = (frame, (1 - self.hi) * 2 + self.core)
        self.sibling = (frame, self.hi * 2 + 1 - self.core)
        self.cross = ((1 - self.lo) * 16 + x * 4 + y, (1 - self.hi) * 2 + self.core)
        self.twin = ((1 - self.lo) * 16 + x * 4 + y, fsdp)
        self.a_next, self.a_prev = self.at(self.ap, self.b), self.at(self.am, self.b)
        self.b_next, self.b_prev = self.at(self.a, self.bp), self.at(self.a, self.bm)

    def at(self, a, b):
        x = a + self.core * (b - a)
        y = b + self.core * (a - b)
        return (self.lo * 16 + x * 4 + y, self.fsdp)


class Copies:
    def __init__(self, send, recv):
        self.send, self.recv, self.count, self.started = send, recv, 0, []

    def start(self, src, dst, device):
        i = self.count
        self.count += 1
        copy = pltpu.make_async_remote_copy(
            src_ref=src, dst_ref=dst, send_sem=self.send.at[i], recv_sem=self.recv.at[i],
            device_id=device, device_id_type=MESH,
        )
        copy.start()
        self.started.append(copy)
        return copy

    def finish(self):
        for copy in self.started:
            copy.wait_send()


def rows_at(index, size):
    return pl.ds(pl.multiple_of(index, size), size)


def exchange_start(here, send, recv, clip, sems):
    recv[clip, here.frame] = send[clip, here.frame]

    @loop(31)
    def _(d):
        peer = lax.rem(here.frame + 1 + d, 32)
        pltpu.make_async_remote_copy(
            src_ref=send.at[clip, peer], dst_ref=recv.at[clip, here.frame],
            send_sem=sems.at[0, clip], recv_sem=sems.at[1, clip],
            device_id=(peer, here.fsdp), device_id_type=MESH,
        ).start()


def exchange_wait(buffer, clip, sem):
    block = buffer.at[clip, pl.ds(0, 31)]
    pltpu.make_async_copy(block, block, sem).wait()


def gather(copies, here, shard, out):
    own = here.fsdp * 256
    base = ((1 - here.hi) * 2 + here.core) * 256
    piece = (here.b * 4 + here.a) * 16
    cross = copies.start(
        shard.at[rows_at(piece, 16), :], out.at[rows_at(own + piece, 16), :], here.cross
    )
    mine = copies.start(shard, out.at[rows_at(own, 256), :], here.sibling)
    yield
    cross.wait_recv()
    block = out.at[rows_at(base + piece, 16), :]
    sent = [copies.start(block, block, here.at(a, here.b)) for a in (here.ap, here.am, here.a2)]
    yield
    for copy in sent:
        copy.wait_recv()
    block = out.at[rows_at(base + here.b * 64, 64), :]
    sent = [copies.start(block, block, here.at(here.a, b)) for b in (here.bp, here.bm, here.b2)]
    over = [copies.start(block, block, here.sibling)]
    yield
    for copy in sent:
        copy.wait_recv()
    for b in (here.bp, here.bm, here.b2):
        block = out.at[rows_at(base + b * 64, 64), :]
        over.append(copies.start(block, block, here.sibling))
    yield
    mine.wait_recv()
    for copy in over:
        copy.wait_recv()


def reduce_chunk(copies, here, s, g, out):
    give, take, held, rb, ra, rz, total = (
        r.at[g] for r in (s.give, s.take, s.held, s.rb, s.ra, s.rz, s.total)
    )
    for h in range(2):
        for i in range(3):
            cols = pl.ds(i * D + g * 256, 256)
            to = pl.ds(i * 256, 256)
            for core, ref in ((1 - here.core, give), (here.core, held)):
                left = s.low_t[rows_at((h * 2 + core) * 256, 256), :]
                ref[h, :, to] = dot(left, s.dqkv[:, cols]).astype(BF16)
    over = copies.start(give, take, here.sibling)
    yield
    over.wait_recv()
    for h in range(2):
        held[h] = (held[h].astype(F32) + take[h].astype(F32)).astype(BF16)

    def scatter(size, offset, at, others, device, dst):
        sent = []
        for i, other in enumerate(others):
            block = held.at[:, rows_at(offset + other * size, size), :]
            sent.append(copies.start(block, dst.at[i], device(other)))
        yield
        for copy in sent:
            copy.wait_recv()
        rows = rows_at(offset + at * size, size)
        sum_ = held[:, rows, :].astype(F32)
        for i in range(3):
            sum_ = sum_ + dst[i].astype(F32)
        held[:, rows, :] = sum_.astype(BF16)

    base = here.b * 64
    yield from scatter(
        64, 0, here.b, (here.bp, here.b2, here.bm), lambda b: here.at(here.a, b), rb
    )
    yield from scatter(
        16, base, here.a, (here.ap, here.a2, here.am), lambda a: here.at(a, here.b), ra
    )

    mine = rows_at(base + here.a * 16, 16)
    slot = here.lo * 2 + here.hi
    rz[slot] = held[here.hi, mine, :]
    sent = [
        copies.start(held.at[1 - here.hi, mine, :], rz.at[slot], here.cross),
        copies.start(held.at[1 - here.hi, mine, :], rz.at[slot], here.far),
        copies.start(held.at[here.hi, mine, :], rz.at[slot], here.twin),
    ]
    yield
    for copy in sent:
        copy.wait_recv()
    sum_ = rz[0].astype(F32)
    for i in range(1, 4):
        sum_ = sum_ + rz[i].astype(F32)
    total[mine, :] = sum_.astype(BF16)

    block = total.at[mine, :]
    sent = [copies.start(block, block, here.at(a, here.b)) for a in (here.ap, here.am, here.a2)]
    yield
    for copy in sent:
        copy.wait_recv()
    block = total.at[rows_at(base, 64), :]
    sent = [copies.start(block, block, here.at(here.a, b)) for b in (here.bp, here.bm, here.b2)]
    yield
    for copy in sent:
        copy.wait_recv()
    for i in range(3):
        out[:, pl.ds(i * D + g * 256, 256)] = total[:, pl.ds(i * 256, 256)].astype(F32)


def kernel(names, *refs):
    s = Scratch(zip(names, refs))
    here = Place()
    loads = {}
    for i, (src, dst) in enumerate((
        (s.x_hbm, s.x),
        (s.sp_qkv, s.wsq.at[rows_at(here.fsdp * 256, 256), :]),
        (s.sp_out, s.wso.at[rows_at(here.fsdp * 256, 256), :]),
        (s.tm_qkv, s.wtq.at[rows_at(here.fsdp * 256, 256), :]),
        (s.tm_out, s.wto.at[rows_at(here.fsdp * 256, 256), :]),
        (s.cot_hbm, s.cot),
    )):
        loads[i] = pltpu.make_async_copy(src, dst, s.local.at[i])
        loads[i].start()

    barrier = pltpu.get_barrier_semaphore()

    @loop(31)
    def _(d):
        peer = lax.rem(here.frame + 1 + d, 32)
        pl.semaphore_signal(barrier, inc=1, device_id=(peer, here.fsdp), device_id_type=MESH)

    for device in (here.sibling, here.cross, here.far):
        pl.semaphore_signal(barrier, inc=1, device_id=device, device_id_type=MESH)
    pl.semaphore_wait(barrier, 34)

    copies = Copies(s.send, s.recv)
    thirds = [pl.ds(i * D, D) for i in range(3)]
    sp = [gather(copies, here, s.sp_qkv.at[:, c], s.wsq.at[:, c]) for c in thirds]
    sp.append(gather(copies, here, s.sp_out, s.wso))
    tm = [gather(copies, here, s.tm_qkv, s.wtq), gather(copies, here, s.tm_out, s.wto)]

    def pump(active, times=1):
        for _ in range(times):
            for steps in active:
                next(steps, None)

    def drain(steps):
        for _ in steps:
            pass

    pump(sp)
    loads[0].wait()

    @loop(8)
    def _(r):
        rows = ds(r, 64)
        s.nrm[rows, :] = normalize(s.x[rows, :].astype(F32))[0].astype(BF16)

    row = lax.broadcasted_iota(jnp.int32, (CLIP, CLIP), 0)
    col = lax.broadcasted_iota(jnp.int32, (CLIP, CLIP), 1)
    allowed = (col <= row) & (((row - col) & 7) == 0)
    s.bias[...] = jnp.where(allowed, 0.0, -1e30)

    pump(sp, 3)
    loads[1].wait()
    for i in range(3):
        drain(sp[i])
        if i == 1:
            pump(tm)

        @loop(2)
        def _(n):
            cols = pl.ds(pl.multiple_of(i * D + n * 512, 512), 512)
            s.qkv[:, cols] = dot(s.nrm[...], s.wsq[:, cols]).astype(BF16)

    pump(tm)
    drain(sp[3])
    loads[2].wait()
    for c in range(2):
        rows = pl.ds(c * CLIP, CLIP)

        @loop(4)
        def _(n):
            for j in range(2):
                q, k, v = (s.qkv[rows, part(i, 2 * n + j)] for i in range(3))
                low = softmax(dot_nt(q, k) * SCALE).astype(BF16)
                s.att[rows, part(0, 2 * n + j)] = dot(low, v).astype(BF16)

        pump(tm)

        @loop(4)
        def _(n):
            cols = ds(n, 256)
            out = dot(s.att[rows, :], s.wso[:, cols]) + s.x[rows, cols].astype(F32)
            s.send_s[c, :, :, cols] = out.reshape(32, 8, 256).astype(BF16)

        exchange_start(here, s.send_s, s.recv_s, c, s.sem_s)

    for steps in tm[::-1]:
        drain(steps)
    for i in (3, 4, 5):
        loads[i].wait()

    @loop(2)
    def _(n):
        cols = ds(n, 512)
        s.da[:, cols] = dot_nt(s.cot[...], s.wto[cols, :]).astype(BF16)

    for c in range(2):
        exchange_wait(s.recv_s, c, s.sem_s.at[1, c])

        @loop(4)
        def _(r):
            rows = rows_at(c * CLIP + r * 64, 64)
            u = s.recv_s[c, ds(r, 8)].astype(F32).reshape(64, D)
            s.low[rows, :] = normalize(u)[0].astype(BF16)

        rows = pl.ds(c * CLIP, CLIP)
        s.low_t[:, rows] = s.low[rows, :].T

        @loop(6)
        def _(n):
            cols = ds(n, 512)
            s.tqkv[rows, cols] = dot(s.low[rows, :], s.wtq[:, cols]).astype(BF16)

    reducing = []
    for g in range(4):

        @loop(2)
        def _(n):
            h = g * 2 + n
            for c in range(2):
                rows = pl.ds(c * CLIP, CLIP)
                q, k, v = (s.tqkv[rows, part(i, h)] for i in range(3))
                probs = softmax(dot_nt(q, k) * SCALE + s.bias[...])
                low = probs.astype(BF16)
                s.att[rows, part(0, h)] = dot(low, v).astype(BF16)
                parts = attend_back(q, k, v, probs, low, s.da[rows, part(0, h)])
                for i in range(3):
                    s.dqkv[rows, part(i, h)] = parts[i].astype(BF16)

        pump(reducing)
        reducing.append(reduce_chunk(copies, here, s, g, s.gtm))
        pump(reducing[-1:])

    for c in range(2):
        rows = pl.ds(c * CLIP, CLIP)

        @loop(4)
        def _(n):
            cols = ds(n, 256)
            s.gin[rows, cols] = dot_nt(s.dqkv[rows, :], s.wtq[cols, :])

        @loop(4)
        def _(r):
            rows = rows_at(c * CLIP + r * 64, 64)
            normed, rstd = normalize(s.recv_s[c, ds(r, 8)].astype(F32).reshape(64, D))
            grad = s.cot[rows, :].astype(F32) + norm_back(normed, rstd, s.gin[rows, :])
            s.send_d[c, ds(r, 8)] = grad.reshape(8, 8, D).astype(BF16)

        exchange_start(here, s.send_d, s.recv_d, c, s.sem_d)
        pump(reducing)

    for c in range(2):

        @loop(2)
        def _(n):
            cols = ds(n, 512)
            rows = pl.ds(c * CLIP, CLIP)
            stream = s.recv_s[c, :, :, cols].astype(F32).reshape(CLIP, 512)
            s.block_out[rows, cols] = (dot(s.att[rows, :], s.wto[:, cols]) + stream).astype(BF16)

    pump(reducing)
    for c in range(2):
        rows = pl.ds(c * CLIP, CLIP)
        exchange_wait(s.recv_d, c, s.sem_d.at[1, c])

        @loop(4)
        def _(r):
            rows = rows_at(c * CLIP + r * 64, 64)
            s.low[rows, :] = s.recv_d[c, ds(r, 8)].astype(F32).reshape(64, D).astype(BF16)

        @loop(2)
        def _(n):
            cols = ds(n, 512)
            s.da[rows, cols] = dot_nt(s.low[rows, :], s.wso[cols, :]).astype(BF16)

        for g in range(2):

            @loop(4)
            def _(n):
                h = g * 4 + n
                q, k, v = (s.qkv[rows, part(i, h)] for i in range(3))
                probs = softmax(dot_nt(q, k) * SCALE)
                parts = attend_back(q, k, v, probs, probs.astype(BF16), s.da[rows, part(0, h)])
                for i in range(3):
                    s.tqkv[rows, part(i, h)] = parts[i].astype(BF16)

            pump(reducing)

        @loop(4)
        def _(n):
            cols = ds(n, 256)
            s.gin[rows, cols] = dot_nt(s.tqkv[rows, :], s.wsq[cols, :])

        pump(reducing)

        @loop(4)
        def _(r):
            rows = rows_at(c * CLIP + r * 64, 64)
            normed, rstd = normalize(s.x[rows, :].astype(F32))
            s.gin[rows, :] = s.low[rows, :].astype(F32) + norm_back(normed, rstd, s.gin[rows, :])

    while reducing:
        pump(reducing)
        reducing = [r for r in reducing if r.gi_frame is not None]
    copies.finish()
    for c in range(2):
        exchange_wait(s.send_s, c, s.sem_s.at[0, c])
        exchange_wait(s.send_d, c, s.sem_d.at[0, c])


class Scratch:
    def __init__(self, pairs):
        for name, ref in pairs:
            setattr(self, name, ref)


VM = pl.BlockSpec(memory_space=pltpu.VMEM)
ANY = pl.BlockSpec(memory_space=pl.ANY)


def body(frames_in, sp_qkv, sp_out, tm_qkv, tm_out, cotangent):
    low = lambda *shape: pltpu.VMEM(shape, BF16)
    dma = pltpu.SemaphoreType.DMA
    scratch = dict(
        x=low(T, D), cot=low(T, D), wsq=low(D, 3 * D), wso=low(D, D), wtq=low(D, 3 * D), wto=low(D, D),
        nrm=low(T, D), qkv=low(T, 3 * D), att=low(T, D), low=low(T, D), low_t=low(D, T),
        tqkv=low(T, 3 * D), da=low(T, D), dqkv=low(T, 3 * D), bias=pltpu.VMEM((CLIP, CLIP), F32),
        send_s=low(2, 32, 8, D), recv_s=low(2, 32, 8, D),
        send_d=low(2, 32, 8, D), recv_d=low(2, 32, 8, D),
        give=low(4, 2, 256, 768), take=low(4, 2, 256, 768), held=low(4, 2, 256, 768),
        rb=low(4, 3, 2, 64, 768), ra=low(4, 3, 2, 16, 768), rz=low(4, 4, 16, 768),
        total=low(4, 256, 768),
        local=dma((6,)), send=dma((COPIES,)), recv=dma((COPIES,)), sem_s=dma((2, 2)), sem_d=dma((2, 2)),
    )
    names = ["x_hbm", "sp_qkv", "sp_out", "tm_qkv", "tm_out", "cot_hbm", "block_out", "gin", "gtm"]
    block_out, grad_in, grad_tm = pl.pallas_call(
        functools.partial(kernel, names + list(scratch)),
        out_shape=[
            jax.ShapeDtypeStruct((T, D), BF16),
            jax.ShapeDtypeStruct((T, D), F32),
            jax.ShapeDtypeStruct((256, 3 * D), F32),
        ],
        in_specs=[ANY] * 6,
        out_specs=[VM] * 3,
        scratch_shapes=list(scratch.values()),
        compiler_params=pltpu.CompilerParams(
            vmem_limit_bytes=VMEM_LIMIT, collective_id=0, has_side_effects=True
        ),
        name="block",
    )(frames_in.reshape(T, D), sp_qkv, sp_out, tm_qkv, tm_out, cotangent.reshape(T, D))
    return (block_out.reshape(cotangent.shape), grad_in.reshape(frames_in.shape), grad_tm)


COPIES = 6 * 12 + 4 * 16


def solution(mesh):
    in_specs = (
        P("fsdp", "frame", None, None),
        P("fsdp", None),
        P("fsdp", None),
        P("fsdp", None),
        P("fsdp", None),
        P("fsdp", None, "frame", None),
    )
    out_specs = (P("fsdp", None, "frame", None), P("fsdp", "frame", None, None), P("fsdp", None))
    return jax.shard_map(body, mesh=mesh, in_specs=in_specs, out_specs=out_specs, check_vma=False)
```

```python
import functools

import jax
import jax.numpy as jnp
from jax import lax
from jax.experimental import pallas as pl
from jax.experimental.pallas import tpu as pltpu
from jax.sharding import PartitionSpec as P

MESH = pl.DeviceIdType.MESH
F32 = jnp.float32
BF16 = jnp.bfloat16
EPS = 1e-05
HEADS = 8
HEAD = 128
SCALE = HEAD**-0.5
D = 1024
T = 512
CLIP = 256
VMEM_LIMIT = 60 * 1024 * 1024


def dot(left, right):
    return lax.dot_general(left, right, (((1,), (0,)), ((), ())), preferred_element_type=F32)


def dot_nt(left, right):
    return lax.dot_general(left, right, (((1,), (1,)), ((), ())), preferred_element_type=F32)


def dot_tn(left, right):
    return lax.dot_general(left, right, (((0,), (0,)), ((), ())), preferred_element_type=F32)


def ds(index, size):
    return pl.ds(pl.multiple_of(index * size, size), size)


def loop(count, unroll=1):
    def run(body):
        def step(i, carry):
            body(i)
            return carry

        lax.fori_loop(0, count, step, 0, unroll=unroll)

    return run


def normalize(u):
    mean = jnp.mean(u, axis=-1, keepdims=True)
    cent = u - mean
    rstd = lax.rsqrt(jnp.mean(cent * cent, axis=-1, keepdims=True) + EPS)
    return cent * rstd, rstd


def norm_back(normed, rstd, grad):
    first = jnp.mean(grad, axis=-1, keepdims=True)
    second = jnp.mean(grad * normed, axis=-1, keepdims=True)
    return rstd * (grad - first - normed * second)


def softmax(scores):
    top = jnp.max(scores, axis=-1, keepdims=True)
    expo = jnp.exp(scores - top)
    return expo / jnp.sum(expo, axis=-1, keepdims=True)


def part(i, head):
    return pl.ds(pl.multiple_of((i * HEADS + head) * HEAD, HEAD), HEAD)


def attention(units, qkv, bias=None, att=None, d_att=None, d_qkv=None):
    q, k, v = ([qkv[rows, part(i, head)] for rows, head in units] for i in range(3))
    n = range(len(units))
    scores = [dot_nt(q[i], k[i]) * SCALE for i in n]
    if d_att is not None:
        a = [d_att[rows, part(0, head)] for rows, head in units]
        d_probs = [dot_nt(a[i], v[i]) for i in n]
    if bias is not None:
        scores = [scores[i] + bias[...] for i in n]
    probs = [softmax(scores[i]) for i in n]
    low = [probs[i].astype(BF16) for i in n]
    if att is not None:
        for i, (rows, head) in enumerate(units):
            att[rows, part(0, head)] = dot(low[i], v[i]).astype(BF16)
    if d_att is None:
        return
    for i, (rows, head) in enumerate(units):
        d_qkv[rows, part(2, head)] = dot_tn(low[i], a[i]).astype(BF16)
    prod = [d_probs[i] * probs[i] for i in n]
    d_s = [
        ((prod[i] - probs[i] * jnp.sum(prod[i], axis=-1, keepdims=True)) * SCALE).astype(BF16)
        for i in n
    ]
    for i, (rows, head) in enumerate(units):
        d_qkv[rows, part(0, head)] = dot(d_s[i], k[i]).astype(BF16)
    for i, (rows, head) in enumerate(units):
        d_qkv[rows, part(1, head)] = dot_tn(d_s[i], q[i]).astype(BF16)


def rows_at(index, size):
    return pl.ds(pl.multiple_of(index, size), size)


class Place:
    def __init__(self):
        frame, fsdp = lax.axis_index("frame"), lax.axis_index("fsdp")
        self.lo, x, y = lax.div(frame, 16), lax.rem(lax.div(frame, 4), 4), lax.rem(frame, 4)
        self.hi, self.core = lax.div(fsdp, 2), lax.rem(fsdp, 2)
        self.x, self.y = x, y
        self.a = x + self.core * (y - x)
        self.b = y + self.core * (x - y)
        self.ap, self.am = lax.rem(self.a + 1, 4), lax.rem(self.a + 3, 4)
        self.bp, self.bm = lax.rem(self.b + 1, 4), lax.rem(self.b + 3, 4)
        self.a2, self.b2 = lax.rem(self.a + 2, 4), lax.rem(self.b + 2, 4)
        self.fsdp, self.frame = fsdp, frame
        self.far = (frame, (1 - self.hi) * 2 + self.core)
        self.sibling = (frame, self.hi * 2 + 1 - self.core)
        self.cross = ((1 - self.lo) * 16 + x * 4 + y, (1 - self.hi) * 2 + self.core)
        self.twin = ((1 - self.lo) * 16 + x * 4 + y, fsdp)
        self.a_next, self.a_prev = self.at(self.ap, self.b), self.at(self.am, self.b)
        self.b_next, self.b_prev = self.at(self.a, self.bp), self.at(self.a, self.bm)

    def across(self, a):
        frame, _ = self.at(a, self.b)
        return (frame + (1 - 2 * self.lo) * 16, (1 - self.hi) * 2 + self.core)

    def at(self, a, b):
        x = a + self.core * (b - a)
        y = b + self.core * (a - b)
        return (self.lo * 16 + x * 4 + y, self.fsdp)


class Copies:
    def __init__(self, send, recv):
        self.send, self.recv, self.count, self.started = send, recv, 0, []

    def start(self, src, dst, device):
        i = self.count
        self.count += 1
        copy = pltpu.make_async_remote_copy(
            src_ref=src, dst_ref=dst, send_sem=self.send.at[i], recv_sem=self.recv.at[i],
            device_id=device, device_id_type=MESH,
        )
        copy.start()
        self.started.append(copy)
        return copy

    def finish(self):
        for copy in self.started:
            copy.wait_send()


def exchange_start(here, send, recv, clip, sems):
    recv[clip, here.frame] = send[clip, here.frame]

    @loop(31)
    def _(d):
        peer = lax.rem(here.frame + 1 + d, 32)
        pltpu.make_async_remote_copy(
            src_ref=send.at[clip, peer], dst_ref=recv.at[clip, here.frame],
            send_sem=sems.at[0, clip], recv_sem=sems.at[1, clip],
            device_id=(peer, here.fsdp), device_id_type=MESH,
        ).start()


def exchange_wait(buffer, clip, sem):
    block = buffer.at[clip, pl.ds(0, 31)]
    pltpu.make_async_copy(block, block, sem).wait()


def gather(copies, here, shard, out, wide):
    own = here.fsdp * 256
    base = ((1 - here.hi) * 2 + here.core) * 256
    piece = (here.b * 4 + here.a) * 16
    row = (here.ap, here.am, here.a2)
    src, dst = shard.at[rows_at(piece, 16), :], out.at[rows_at(own + piece, 16), :]
    sent = [copies.start(src, dst, here.cross)]
    if wide:
        sent += [copies.start(src, dst, here.across(a)) for a in row]
    yield
    for copy in sent:
        copy.wait_recv()
    if not wide:
        block = out.at[rows_at(base + piece, 16), :]
        sent = [copies.start(block, block, here.at(a, here.b)) for a in row]
        yield
        for copy in sent:
            copy.wait_recv()
    block = out.at[rows_at(base + here.b * 64, 64), :]
    sent = [copies.start(block, block, here.at(here.a, b)) for b in (here.bp, here.bm, here.b2)]
    over = [copies.start(block, block, here.sibling)]
    yield
    for copy in sent:
        copy.wait_recv()
    for b in (here.bp, here.bm, here.b2):
        block = out.at[rows_at(base + b * 64, 64), :]
        over.append(copies.start(block, block, here.sibling))
    yield
    for copy in over:
        copy.wait_recv()


def gather_across(copies, here, shard, out):
    half = rows_at(here.fsdp * 256 + (1 - here.lo) * 128, 128)
    cross = copies.start(shard.at[rows_at((1 - here.lo) * 128, 128), :], out.at[half, :], here.cross)
    yield
    cross.wait_recv()
    base = ((1 - here.hi) * 2 + here.core) * 256
    block = out.at[rows_at(base + here.lo * 128, 128), :]
    twin = copies.start(block, block, here.twin)
    over = [copies.start(block, block, here.sibling)]
    yield
    twin.wait_recv()
    block = out.at[rows_at(base + (1 - here.lo) * 128, 128), :]
    over.append(copies.start(block, block, here.sibling))
    yield
    for copy in over:
        copy.wait_recv()


def reduce_chunk(copies, here, s, g, across_first):
    give, take, held, rb, ra, rz, total = (
        r.at[g] for r in (s.give, s.take, s.held, s.rb, s.ra, s.rz, s.total)
    )
    for h in range(2):
        for i in range(3):
            cols = pl.ds(i * D + g * 256, 256)
            to = pl.ds(i * 256, 256)
            for core, ref in ((1 - here.core, give), (here.core, held)):
                left = s.low_t[rows_at((h * 2 + core) * 256, 256), :]
                ref[h, :, to] = dot(left, s.dqkv[:, cols]).astype(BF16)
    over = copies.start(give, take, here.sibling)
    yield
    over.wait_recv()
    for h in range(2):
        held[h] = (held[h].astype(F32) + take[h].astype(F32)).astype(BF16)
    shards, count = slice(None), 2
    if across_first:
        rx = s.rx.at[g]
        cross = copies.start(held.at[1 - here.hi], rx, here.cross)
        yield
        cross.wait_recv()
        held[here.hi] = (held[here.hi].astype(F32) + rx[...].astype(F32)).astype(BF16)
        shards, count = pl.ds(here.hi, 1), 1

    def scatter(size, offset, at, others, device, dst):
        sent = []
        for i, other in enumerate(others):
            block = held.at[shards, rows_at(offset + other * size, size), :]
            sent.append(copies.start(block, dst.at[i, pl.ds(0, count)], device(other)))
        yield
        for copy in sent:
            copy.wait_recv()
        rows = rows_at(offset + at * size, size)
        sum_ = held[shards, rows, :].astype(F32)
        for i in range(3):
            sum_ = sum_ + dst[i, :count].astype(F32)
        held[shards, rows, :] = sum_.astype(BF16)

    base = here.b * 64
    yield from scatter(
        64, 0, here.b, (here.bp, here.b2, here.bm), lambda b: here.at(here.a, b), rb
    )
    yield from scatter(
        16, base, here.a, (here.ap, here.a2, here.am), lambda a: here.at(a, here.b), ra
    )

    mine = rows_at(base + here.a * 16, 16)
    own = held.at[here.hi, mine, :]
    if across_first:
        sent = [copies.start(own, rz.at[0], here.twin)]
    else:
        slot = here.lo * 2 + here.hi
        rz[slot] = own[...]
        other = held.at[1 - here.hi, mine, :]
        sent = [copies.start(own, rz.at[slot], here.twin)]
        sent += [copies.start(other, rz.at[slot], to) for to in (here.cross, here.far)]
    yield
    for copy in sent:
        copy.wait_recv()
    sum_ = rz[0].astype(F32)
    if across_first:
        sum_ = sum_ + own[...].astype(F32)
    else:
        for i in range(1, 4):
            sum_ = sum_ + rz[i].astype(F32)
    total[mine, :] = sum_.astype(BF16)

    block = total.at[mine, :]
    sent = [copies.start(block, block, here.at(a, here.b)) for a in (here.ap, here.am, here.a2)]
    yield
    for copy in sent:
        copy.wait_recv()
    block = total.at[rows_at(base, 64), :]
    sent = [copies.start(block, block, here.at(here.a, b)) for b in (here.bp, here.bm, here.b2)]
    yield
    for copy in sent:
        copy.wait_recv()
    for i in range(3):
        s.gtm[:, pl.ds(i * D + g * 256, 256)] = total[:, pl.ds(i * 256, 256)].astype(F32)


def kernel(names, *refs):
    s = Scratch(zip(names, refs))
    here = Place()
    loads = {}
    for i, (src, dst) in enumerate((
        (s.x_hbm, s.x),
        (s.sp_qkv, s.wsq.at[rows_at(here.fsdp * 256, 256), :]),
        (s.sp_out, s.wso.at[rows_at(here.fsdp * 256, 256), :]),
        (s.tm_qkv, s.wtq.at[rows_at(here.fsdp * 256, 256), :]),
        (s.tm_out, s.wto.at[rows_at(here.fsdp * 256, 256), :]),
        (s.cot_hbm, s.cot),
    )):
        loads[i] = pltpu.make_async_copy(src, dst, s.local.at[i])
        loads[i].start()

    barrier = pltpu.get_barrier_semaphore()

    @loop(31)
    def _(d):
        peer = lax.rem(here.frame + 1 + d, 32)
        pl.semaphore_signal(barrier, inc=1, device_id=(peer, here.fsdp), device_id_type=MESH)

    near = [here.sibling, here.cross, here.far]
    for device in near + [here.across(a) for a in (here.ap, here.am, here.a2)]:
        pl.semaphore_signal(barrier, inc=1, device_id=device, device_id_type=MESH)
    copies = Copies(s.sent, s.got)

    def drain(*many):
        for steps in many:
            for _ in steps:
                pass

    def step(*many):
        for steps in many:
            next(steps)

    thirds = [pl.ds(i * D, D) for i in range(3)]
    halves = [[pl.ds(i * D + n * 512, 512) for i in range(3)] for n in range(2)]
    sp = [
        [gather(copies, here, s.sp_qkv.at[:, c], s.wsq.at[:, c], n == 0) for c in halves[n]]
        for n in range(2)
    ]
    sp_out = gather_across(copies, here, s.sp_out, s.wso)
    tm = [gather_across(copies, here, s.tm_qkv.at[:, c], s.wtq.at[:, c]) for c in thirds[:2]]
    tm.append(gather(copies, here, s.tm_qkv.at[:, thirds[2]], s.wtq.at[:, thirds[2]], False))
    tm_out = gather_across(copies, here, s.tm_out, s.wto)

    loads[0].wait()

    @loop(8)
    def _(r):
        rows = ds(r, 64)
        s.low[rows, :] = normalize(s.x[rows, :].astype(F32))[0].astype(BF16)

    pl.semaphore_wait(barrier, 37)
    step(*sp[0], *sp[1])

    def over(shard, out):
        return copies.start(shard, out.at[rows_at(here.fsdp * 256, 256), :], here.sibling)

    mine = [over(s.sp_qkv, s.wsq), over(s.sp_out, s.wso)]
    step(sp_out, tm[2])

    row = lax.broadcasted_iota(jnp.int32, (CLIP, CLIP), 0)
    col = lax.broadcasted_iota(jnp.int32, (CLIP, CLIP), 1)
    allowed = (col <= row) & (((row - col) & 7) == 0)
    s.bias[...] = jnp.where(allowed, 0.0, -1e30)

    step(*sp[0], *sp[1])
    step(*sp[1])
    step(sp_out)
    step(tm[0], tm[1])
    step(*sp[0])
    mine[0].wait_recv()
    loads[1].wait()

    def project(n):
        drain(*sp[n])
        for i in range(3):
            cols = halves[n][i]
            s.qkv[:, cols] = dot(s.low[...], s.wsq[:, cols]).astype(BF16)

    def attend(n):
        @loop(2)
        def _(c):
            rows = rows_at(c * CLIP, CLIP)
            attention([(rows, n * 4 + j) for j in range(4)], s.qkv, att=s.att)

    project(0)
    step(*sp[1])
    step(tm[2])
    attend(0)
    project(1)
    step(sp_out)
    step(tm[2], tm[0], tm[1], tm_out)
    mine += [over(s.tm_qkv, s.wtq), over(s.tm_out, s.wto)]
    attend(1)
    drain(sp_out)
    mine[1].wait_recv()
    loads[2].wait()
    for c in range(2):
        rows = pl.ds(c * CLIP, CLIP)

        @loop(4)
        def _(n):
            cols = ds(n, 256)
            out = dot(s.att[rows, :], s.wso[:, cols]) + s.x[rows, cols].astype(F32)
            s.send[c, :, :, cols] = out.reshape(32, 8, 256).astype(BF16)

        exchange_start(here, s.send, s.recv_s, c, s.sem_s)

    step(tm_out, tm[0], tm[1], tm[2], tm_out)
    drain(*tm, tm_out)
    mine[2].wait_recv()
    mine[3].wait_recv()
    for i in (3, 4, 5):
        loads[i].wait()

    @loop(2)
    def _(n):
        cols = ds(n, 512)
        s.da[:, cols] = dot_nt(s.cot[...], s.wto[cols, :]).astype(BF16)

    for c in range(2):
        exchange_wait(s.recv_s, c, s.sem_s.at[1, c])

        @loop(4)
        def _(r):
            rows = rows_at(c * CLIP + r * 64, 64)
            u = s.recv_s[c, ds(r, 8)].astype(F32).reshape(64, D)
            s.low[rows, :] = normalize(u)[0].astype(BF16)

        rows = pl.ds(c * CLIP, CLIP)
        s.low_t[:, rows] = s.low[rows, :].T

    def pump(*which):
        for g in which:
            next(chunks[g], None)

    chunks = [reduce_chunk(copies, here, s, g, g < 2) for g in range(4)]
    for g in range(4):

        @loop(3)
        def _(i):
            cols = pl.ds(pl.multiple_of(i * D + g * 256, 256), 256)
            s.tqkv[:, cols] = dot(s.low[...], s.wtq[:, cols]).astype(BF16)

        units = [(pl.ds(c * CLIP, CLIP), g * 2 + n) for n in range(2) for c in range(2)]
        attention(units, s.tqkv, s.bias, s.att, s.da, s.dqkv)
        step(chunks[g])
        if g > 0:
            step(chunks[g - 1])

    for c in range(2):
        rows = pl.ds(c * CLIP, CLIP)

        @loop(4)
        def _(n):
            cols = ds(n, 256)
            s.grad[rows, cols] = dot_nt(s.dqkv[rows, :], s.wtq[cols, :])

        pump(*((3, 0), (2,))[c])
        exchange_wait(s.send, c, s.sem_s.at[0, c])

        @loop(4)
        def _(r):
            rows = rows_at(c * CLIP + r * 64, 64)
            normed, rstd = normalize(s.recv_s[c, ds(r, 8)].astype(F32).reshape(64, D))
            grad = s.cot[rows, :].astype(F32) + norm_back(normed, rstd, s.grad[rows, :])
            s.send[c, ds(r, 8)] = grad.reshape(8, 8, D).astype(BF16)

        exchange_start(here, s.send, s.recv_d, c, s.sem_d)

    for c in range(2):

        @loop(2)
        def _(n):
            cols = ds(n, 512)
            rows = pl.ds(c * CLIP, CLIP)
            stream = s.recv_s[c, :, :, cols].astype(F32).reshape(CLIP, 512)
            s.block_out[rows, cols] = (dot(s.att[rows, :], s.wto[:, cols]) + stream).astype(BF16)

        pump(*((0,), (2, 1))[c])

    for c in range(2):
        rows = pl.ds(c * CLIP, CLIP)
        exchange_wait(s.recv_d, c, s.sem_d.at[1, c])

        @loop(4)
        def _(r):
            rows = rows_at(c * CLIP + r * 64, 64)
            s.low[rows, :] = s.recv_d[c, ds(r, 8)].astype(F32).reshape(64, D).astype(BF16)

        @loop(2)
        def _(n):
            cols = ds(n, 512)
            s.da[rows, cols] = dot_nt(s.low[rows, :], s.wso[cols, :]).astype(BF16)

        pump(*((3, 0), ())[c])

        for g in range(2):

            units = [(rows, g * 4 + n) for n in range(4)]
            attention(units, s.qkv, d_att=s.da, d_qkv=s.tqkv)
            pump(*((2,), (1, 3, 0), (1, 3, 2), (0,))[c * 2 + g])

        @loop(4)
        def _(n):
            cols = ds(n, 256)
            s.grad[rows, cols] = dot_nt(s.tqkv[rows, :], s.wsq[cols, :])

        pump(*((2,), (1, 3))[c])

        @loop(4)
        def _(r):
            rows = rows_at(c * CLIP + r * 64, 64)
            normed, rstd = normalize(s.x[rows, :].astype(F32))
            grad = s.low[rows, :].astype(F32) + norm_back(normed, rstd, s.grad[rows, :])
            s.gin[rows, :] = grad.astype(BF16)

        pump(*((3, 1, 0), (1,))[c])

    drain(*chunks)
    copies.finish()
    for c in range(2):
        exchange_wait(s.send, c, s.sem_d.at[0, c])


class Scratch:
    def __init__(self, pairs):
        for name, ref in pairs:
            setattr(self, name, ref)


VM = pl.BlockSpec(memory_space=pltpu.VMEM)
ANY = pl.BlockSpec(memory_space=pl.ANY)


def body(frames_in, sp_qkv, sp_out, tm_qkv, tm_out, cotangent):
    low = lambda *shape: pltpu.VMEM(shape, BF16)
    dma = pltpu.SemaphoreType.DMA
    scratch = dict(
        x=low(T, D), cot=low(T, D), wsq=low(D, 3 * D), wso=low(D, D), wtq=low(D, 3 * D), wto=low(D, D),
        qkv=low(T, 3 * D), att=low(T, D), low=low(T, D), low_t=low(D, T),
        tqkv=low(T, 3 * D), da=low(T, D), dqkv=low(T, 3 * D), bias=pltpu.VMEM((CLIP, CLIP), F32),
        send=low(2, 32, 8, D), recv_s=low(2, 32, 8, D),
        recv_d=low(2, 32, 8, D),
        give=low(4, 2, 256, 768), take=low(4, 2, 256, 768), held=low(4, 2, 256, 768),
        rb=low(4, 3, 2, 64, 768), ra=low(4, 3, 2, 16, 768), rz=low(4, 4, 16, 768),
        total=low(4, 256, 768), rx=low(2, 256, 768), grad=pltpu.VMEM((T, D), F32),
        local=dma((6,)), sent=dma((COPIES,)), got=dma((COPIES,)), sem_s=dma((2, 2)), sem_d=dma((2, 2)),
    )
    names = ["x_hbm", "sp_qkv", "sp_out", "tm_qkv", "tm_out", "cot_hbm", "block_out", "gin", "gtm"]
    block_out, grad_in, grad_tm = pl.pallas_call(
        functools.partial(kernel, names + list(scratch)),
        out_shape=[
            jax.ShapeDtypeStruct((T, D), BF16),
            jax.ShapeDtypeStruct((T, D), BF16),
            jax.ShapeDtypeStruct((256, 3 * D), F32),
        ],
        in_specs=[ANY] * 6,
        out_specs=[VM] * 3,
        scratch_shapes=list(scratch.values()),
        compiler_params=pltpu.CompilerParams(
            vmem_limit_bytes=VMEM_LIMIT, collective_id=0, has_side_effects=True
        ),
        name="block",
    )(frames_in.reshape(T, D), sp_qkv, sp_out, tm_qkv, tm_out, cotangent.reshape(T, D))
    return (block_out.reshape(cotangent.shape), grad_in.reshape(frames_in.shape).astype(F32), grad_tm)


COPIES = 200


def solution(mesh):
    in_specs = (
        P("fsdp", "frame", None, None),
        P("fsdp", None),
        P("fsdp", None),
        P("fsdp", None),
        P("fsdp", None),
        P("fsdp", None, "frame", None),
    )
    out_specs = (P("fsdp", None, "frame", None), P("fsdp", "frame", None, None), P("fsdp", None))
    return jax.shard_map(body, mesh=mesh, in_specs=in_specs, out_specs=out_specs, check_vma=False)
```

```python
import functools

import jax
import jax.numpy as jnp
from jax import lax
from jax.experimental import pallas as pl
from jax.experimental.pallas import tpu as pltpu
from jax.sharding import PartitionSpec as P

MESH = pl.DeviceIdType.MESH
F32 = jnp.float32
BF16 = jnp.bfloat16
EPS = 1e-05
HEADS = 8
HEAD = 128
SCALE = HEAD**-0.5
D = 1024
T = 512
CLIP = 256
VMEM_LIMIT = 60 * 1024 * 1024


def dot(left, right):
    return lax.dot_general(left, right, (((1,), (0,)), ((), ())), preferred_element_type=F32)


def dot_nt(left, right):
    return lax.dot_general(left, right, (((1,), (1,)), ((), ())), preferred_element_type=F32)


def dot_tn(left, right):
    return lax.dot_general(left, right, (((0,), (0,)), ((), ())), preferred_element_type=F32)


def ds(index, size):
    return pl.ds(pl.multiple_of(index * size, size), size)


def loop(count, unroll=1):
    def run(body):
        def step(i, carry):
            body(i)
            return carry

        lax.fori_loop(0, count, step, 0, unroll=unroll)

    return run


def normalize(u):
    mean = jnp.mean(u, axis=-1, keepdims=True)
    cent = u - mean
    rstd = lax.rsqrt(jnp.mean(cent * cent, axis=-1, keepdims=True) + EPS)
    return cent * rstd, rstd


def norm_back(normed, rstd, grad):
    first = jnp.mean(grad, axis=-1, keepdims=True)
    second = jnp.mean(grad * normed, axis=-1, keepdims=True)
    return rstd * (grad - first - normed * second)


def softmax(scores):
    top = jnp.max(scores, axis=-1, keepdims=True)
    expo = jnp.exp(scores - top)
    return expo / jnp.sum(expo, axis=-1, keepdims=True)


def part(i, head):
    return pl.ds(pl.multiple_of((i * HEADS + head) * HEAD, HEAD), HEAD)


def attention(units, qkv, bias=None, att=None, d_att=None, d_qkv=None):
    q, k, v = ([qkv[rows, part(i, head)] for rows, head in units] for i in range(3))
    n = range(len(units))
    scores = [dot_nt(q[i], k[i]) * SCALE for i in n]
    if d_att is not None:
        a = [d_att[rows, part(0, head)] for rows, head in units]
        d_probs = [dot_nt(a[i], v[i]) for i in n]
    if bias is not None:
        scores = [scores[i] + bias[...] for i in n]
    probs = [softmax(scores[i]) for i in n]
    low = [probs[i].astype(BF16) for i in n]
    if att is not None:
        for i, (rows, head) in enumerate(units):
            att[rows, part(0, head)] = dot(low[i], v[i]).astype(BF16)
    if d_att is None:
        return
    for i, (rows, head) in enumerate(units):
        d_qkv[rows, part(2, head)] = dot_tn(low[i], a[i]).astype(BF16)
    prod = [d_probs[i] * probs[i] for i in n]
    d_s = [
        ((prod[i] - probs[i] * jnp.sum(prod[i], axis=-1, keepdims=True)) * SCALE).astype(BF16)
        for i in n
    ]
    for i, (rows, head) in enumerate(units):
        d_qkv[rows, part(0, head)] = dot(d_s[i], k[i]).astype(BF16)
    for i, (rows, head) in enumerate(units):
        d_qkv[rows, part(1, head)] = dot_tn(d_s[i], q[i]).astype(BF16)


def rows_at(index, size):
    return pl.ds(pl.multiple_of(index, size), size)


class Place:
    def __init__(self):
        frame, fsdp = lax.axis_index("frame"), lax.axis_index("fsdp")
        self.lo, x, y = lax.div(frame, 16), lax.rem(lax.div(frame, 4), 4), lax.rem(frame, 4)
        self.hi, self.core = lax.div(fsdp, 2), lax.rem(fsdp, 2)
        self.x, self.y = x, y
        self.a = x + self.core * (y - x)
        self.b = y + self.core * (x - y)
        self.ap, self.am = lax.rem(self.a + 1, 4), lax.rem(self.a + 3, 4)
        self.bp, self.bm = lax.rem(self.b + 1, 4), lax.rem(self.b + 3, 4)
        self.a2, self.b2 = lax.rem(self.a + 2, 4), lax.rem(self.b + 2, 4)
        self.fsdp, self.frame = fsdp, frame
        self.far = (frame, (1 - self.hi) * 2 + self.core)
        self.sibling = (frame, self.hi * 2 + 1 - self.core)
        self.cross = ((1 - self.lo) * 16 + x * 4 + y, (1 - self.hi) * 2 + self.core)
        self.twin = ((1 - self.lo) * 16 + x * 4 + y, fsdp)
        self.a_next, self.a_prev = self.at(self.ap, self.b), self.at(self.am, self.b)
        self.b_next, self.b_prev = self.at(self.a, self.bp), self.at(self.a, self.bm)

    def at(self, a, b):
        x = a + self.core * (b - a)
        y = b + self.core * (a - b)
        return (self.lo * 16 + x * 4 + y, self.fsdp)


class Copies:
    def __init__(self, send, recv):
        self.send, self.recv, self.count, self.started = send, recv, 0, []

    def start(self, src, dst, device):
        i = self.count
        self.count += 1
        copy = pltpu.make_async_remote_copy(
            src_ref=src, dst_ref=dst, send_sem=self.send.at[i], recv_sem=self.recv.at[i],
            device_id=device, device_id_type=MESH,
        )
        copy.start()
        self.started.append(copy)
        return copy

    def finish(self):
        for copy in self.started:
            copy.wait_send()


def exchange_start(here, send, recv, clip, sems):
    recv[clip, here.frame] = send[clip, here.frame]

    @loop(31)
    def _(d):
        peer = lax.rem(here.frame + 1 + d, 32)
        pltpu.make_async_remote_copy(
            src_ref=send.at[clip, peer], dst_ref=recv.at[clip, here.frame],
            send_sem=sems.at[0, clip], recv_sem=sems.at[1, clip],
            device_id=(peer, here.fsdp), device_id_type=MESH,
        ).start()


def exchange_wait(buffer, clip, sem):
    block = buffer.at[clip, pl.ds(0, 31)]
    pltpu.make_async_copy(block, block, sem).wait()


def gather(copies, here, shard, out):
    own = here.fsdp * 256
    base = ((1 - here.hi) * 2 + here.core) * 256
    piece = (here.b * 4 + here.a) * 16
    row = (here.ap, here.am, here.a2)
    src, dst = shard.at[rows_at(piece, 16), :], out.at[rows_at(own + piece, 16), :]
    cross = copies.start(src, dst, here.cross)
    yield
    cross.wait_recv()
    block = out.at[rows_at(base + piece, 16), :]
    sent = [copies.start(block, block, here.at(a, here.b)) for a in row]
    yield
    for copy in sent:
        copy.wait_recv()
    block = out.at[rows_at(base + here.b * 64, 64), :]
    sent = [copies.start(block, block, here.at(here.a, b)) for b in (here.bp, here.bm, here.b2)]
    over = [copies.start(block, block, here.sibling)]
    yield
    for copy in sent:
        copy.wait_recv()
    for b in (here.bp, here.bm, here.b2):
        block = out.at[rows_at(base + b * 64, 64), :]
        over.append(copies.start(block, block, here.sibling))
    yield
    for copy in over:
        copy.wait_recv()


def gather_whole(copies, here, shard, out):
    own = rows_at(here.fsdp * 256, 256)
    cross = copies.start(shard, out.at[own, :], here.cross)
    yield
    cross.wait_recv()
    block = out.at[rows_at(((1 - here.hi) * 2 + here.core) * 256, 256), :]
    over = copies.start(block, block, here.sibling)
    yield
    over.wait_recv()


def gather_across(copies, here, shard, out):
    half = rows_at(here.fsdp * 256 + (1 - here.lo) * 128, 128)
    cross = copies.start(shard.at[rows_at((1 - here.lo) * 128, 128), :], out.at[half, :], here.cross)
    yield
    cross.wait_recv()
    base = ((1 - here.hi) * 2 + here.core) * 256
    block = out.at[rows_at(base + here.lo * 128, 128), :]
    twin = copies.start(block, block, here.twin)
    over = [copies.start(block, block, here.sibling)]
    yield
    twin.wait_recv()
    block = out.at[rows_at(base + (1 - here.lo) * 128, 128), :]
    over.append(copies.start(block, block, here.sibling))
    yield
    for copy in over:
        copy.wait_recv()


def reduce_chunk(copies, here, s, g, across_first):
    give, take, held, rb, ra, rz, total = (
        r.at[g] for r in (s.give, s.take, s.held, s.rb, s.ra, s.rz, s.total)
    )
    for h in range(2):
        for i in range(3):
            cols = pl.ds(i * D + g * 256, 256)
            to = pl.ds(i * 256, 256)
            for core, ref in ((1 - here.core, give), (here.core, held)):
                left = s.low_t[rows_at((h * 2 + core) * 256, 256), :]
                ref[h, :, to] = dot(left, s.dqkv[:, cols]).astype(BF16)
    over = copies.start(give, take, here.sibling)
    yield
    over.wait_recv()
    for h in range(2):
        held[h] = (held[h].astype(F32) + take[h].astype(F32)).astype(BF16)
    shards, count = slice(None), 2
    if across_first:
        rx = s.rx.at[sum(ACROSS_FIRST[:g])]
        cross = copies.start(held.at[1 - here.hi], rx, here.cross)
        yield
        cross.wait_recv()
        held[here.hi] = (held[here.hi].astype(F32) + rx[...].astype(F32)).astype(BF16)
        shards, count = pl.ds(here.hi, 1), 1

    def scatter(size, offset, at, others, device, dst):
        sent = []
        for i, other in enumerate(others):
            block = held.at[shards, rows_at(offset + other * size, size), :]
            sent.append(copies.start(block, dst.at[i, pl.ds(0, count)], device(other)))
        yield
        for copy in sent:
            copy.wait_recv()
        rows = rows_at(offset + at * size, size)
        sum_ = held[shards, rows, :].astype(F32)
        for i in range(3):
            sum_ = sum_ + dst[i, :count].astype(F32)
        held[shards, rows, :] = sum_.astype(BF16)

    base = here.b * 64
    yield from scatter(
        64, 0, here.b, (here.bp, here.b2, here.bm), lambda b: here.at(here.a, b), rb
    )
    yield from scatter(
        16, base, here.a, (here.ap, here.a2, here.am), lambda a: here.at(a, here.b), ra
    )

    mine = rows_at(base + here.a * 16, 16)
    own = held.at[here.hi, mine, :]
    if across_first:
        sent = [copies.start(own, rz.at[0], here.twin)]
    else:
        slot = here.lo * 2 + here.hi
        rz[slot] = own[...]
        other = held.at[1 - here.hi, mine, :]
        sent = [copies.start(own, rz.at[slot], here.twin)]
        sent += [copies.start(other, rz.at[slot], to) for to in (here.cross, here.far)]
    yield
    for copy in sent:
        copy.wait_recv()
    sum_ = rz[0].astype(F32)
    if across_first:
        sum_ = sum_ + own[...].astype(F32)
    else:
        for i in range(1, 4):
            sum_ = sum_ + rz[i].astype(F32)
    total[mine, :] = sum_.astype(BF16)

    block = total.at[mine, :]
    sent = [copies.start(block, block, here.at(a, here.b)) for a in (here.ap, here.am, here.a2)]
    yield
    for copy in sent:
        copy.wait_recv()
    block = total.at[rows_at(base, 64), :]
    sent = [copies.start(block, block, here.at(here.a, b)) for b in (here.bp, here.bm, here.b2)]
    yield
    for copy in sent:
        copy.wait_recv()
    for i in range(3):
        cols = pl.ds(i * D + g * 256, 256)
        s.gtm[:, cols] = total[:, pl.ds(i * 256, 256)].astype(F32)
        pltpu.make_async_copy(s.gtm.at[:, cols], s.gtm_out.at[:, cols], s.local.at[6 + g * 3 + i]).start()


def kernel(names, *refs):
    s = Scratch(zip(names, refs))
    here = Place()
    loads = {}
    for i, (src, dst) in enumerate((
        (s.x_hbm, s.x),
        (s.sp_qkv, s.wsq.at[rows_at(here.fsdp * 256, 256), :]),
        (s.sp_out, s.wso.at[rows_at(here.fsdp * 256, 256), :]),
        (s.tm_qkv, s.wtq.at[rows_at(here.fsdp * 256, 256), :]),
        (s.tm_out, s.wto.at[rows_at(here.fsdp * 256, 256), :]),
        (s.cot_hbm, s.cot),
    )):
        loads[i] = pltpu.make_async_copy(src, dst, s.local.at[i])
        loads[i].start()

    barrier = pltpu.get_barrier_semaphore()

    @loop(31)
    def _(d):
        peer = lax.rem(here.frame + 1 + d, 32)
        pl.semaphore_signal(barrier, inc=1, device_id=(peer, here.fsdp), device_id_type=MESH)

    for device in (here.sibling, here.cross, here.far):
        pl.semaphore_signal(barrier, inc=1, device_id=device, device_id_type=MESH)
    copies = Copies(s.sent, s.got)

    def drain(*many):
        for steps in many:
            for _ in steps:
                pass

    def step(*many):
        for steps in many:
            next(steps)

    thirds = [pl.ds(i * D, D) for i in range(3)]
    halves = [[pl.ds(i * D + n * 512, 512) for i in range(3)] for n in range(2)]
    sp = [
        [gather(copies, here, s.sp_qkv.at[:, c], s.wsq.at[:, c]) for c in halves[n]]
        for n in range(2)
    ]
    sp_out = gather_across(copies, here, s.sp_out, s.wso)
    tm = [
        how(copies, here, s.tm_qkv.at[:, c], s.wtq.at[:, c])
        for how, c in zip((gather, gather_across, gather), thirds)
    ]
    tm_out = gather_whole(copies, here, s.tm_out, s.wto)

    loads[0].wait()

    @loop(8)
    def _(r):
        rows = ds(r, 64)
        s.low[rows, :] = normalize(s.x[rows, :].astype(F32))[0].astype(BF16)

    pl.semaphore_wait(barrier, 34)
    step(*sp[0], *sp[1])

    def over(shard, out):
        return copies.start(shard, out.at[rows_at(here.fsdp * 256, 256), :], here.sibling)

    mine = [over(s.sp_qkv, s.wsq), over(s.sp_out, s.wso)]
    step(sp_out, *tm)

    row = lax.broadcasted_iota(jnp.int32, (CLIP, CLIP), 0)
    col = lax.broadcasted_iota(jnp.int32, (CLIP, CLIP), 1)
    allowed = (col <= row) & (((row - col) & 7) == 0)
    s.bias[...] = jnp.where(allowed, 0.0, -1e30)

    step(*sp[0], *sp[1])
    step(*sp[0])
    step(*sp[1])
    step(sp_out, tm_out)
    step(tm[0], tm[2])
    step(*sp[0])
    mine[0].wait_recv()
    loads[1].wait()

    def project(n):
        drain(*sp[n])
        for i in range(3):
            cols = halves[n][i]
            s.qkv[:, cols] = dot(s.low[...], s.wsq[:, cols]).astype(BF16)

    def attend(n, c):
        rows = pl.ds(c * CLIP, CLIP)
        attention([(rows, n * 4 + j) for j in range(4)], s.qkv, att=s.att)

    project(0)
    step(*sp[1])
    step(tm[0], tm[2], tm[1])
    attend(0, 0)
    attend(0, 1)
    project(1)
    step(sp_out)
    mine += [over(s.tm_qkv, s.wtq), over(s.tm_out, s.wto)]
    for c in range(2):
        attend(1, c)
        if c == 0:
            drain(sp_out)
            mine[1].wait_recv()
            loads[2].wait()
        rows = pl.ds(c * CLIP, CLIP)

        @loop(4)
        def _(n):
            cols = ds(n, 256)
            out = dot(s.att[rows, :], s.wso[:, cols]) + s.x[rows, cols].astype(F32)
            s.send[c, :, :, cols] = out.reshape(32, 8, 256).astype(BF16)

        exchange_start(here, s.send, s.recv_s, c, s.sem_s)

    step(tm_out)
    step(*tm)
    drain(*tm, tm_out)
    mine[2].wait_recv()
    mine[3].wait_recv()
    for i in (3, 4, 5):
        loads[i].wait()

    @loop(2)
    def _(n):
        cols = ds(n, 512)
        s.da[:, cols] = dot_nt(s.cot[...], s.wto[cols, :]).astype(BF16)

    for c in range(2):
        exchange_wait(s.recv_s, c, s.sem_s.at[1, c])

        @loop(4)
        def _(r):
            rows = rows_at(c * CLIP + r * 64, 64)
            u = s.recv_s[c, ds(r, 8)].astype(F32).reshape(64, D)
            s.low[rows, :] = normalize(u)[0].astype(BF16)

        rows = pl.ds(c * CLIP, CLIP)
        s.low_t[:, rows] = s.low[rows, :].T
        if c == 0:

            @loop(6)
            def _(n):
                cols = ds(n, 512)
                s.tqkv[:CLIP, cols] = dot(s.low[:CLIP, :], s.wtq[:, cols]).astype(BF16)

    def pump(point):
        for g in PLAN.get(point, ()):
            next(chunks[g], None)

    chunks = [reduce_chunk(copies, here, s, g, ACROSS_FIRST[g]) for g in range(4)]
    for g in range(4):

        for i in range(3):
            cols = pl.ds(i * D + g * 256, 256)
            s.tqkv[CLIP:, cols] = dot(s.low[CLIP:, :], s.wtq[:, cols]).astype(BF16)

        units = [(pl.ds(c * CLIP, CLIP), g * 2 + n) for n in range(2) for c in range(2)]
        attention(units, s.tqkv, s.bias, s.att, s.da, s.dqkv)
        step(chunks[g])
        pump(f"group{g}")

    for c in range(2):
        rows = pl.ds(c * CLIP, CLIP)

        @loop(4)
        def _(n):
            cols = ds(n, 256)
            s.grad[rows, cols] = dot_nt(s.dqkv[rows, :], s.wtq[cols, :])

        pump(f"grad{c}")
        exchange_wait(s.send, c, s.sem_s.at[0, c])

        @loop(4)
        def _(r):
            rows = rows_at(c * CLIP + r * 64, 64)
            normed, rstd = normalize(s.recv_s[c, ds(r, 8)].astype(F32).reshape(64, D))
            grad = s.cot[rows, :].astype(F32) + norm_back(normed, rstd, s.grad[rows, :])
            s.send[c, ds(r, 8)] = grad.reshape(8, 8, D).astype(BF16)

        exchange_start(here, s.send, s.recv_d, c, s.sem_d)

    for c in range(2):

        @loop(2)
        def _(n):
            cols = ds(n, 512)
            rows = pl.ds(c * CLIP, CLIP)
            stream = s.recv_s[c, :, :, cols].astype(F32).reshape(CLIP, 512)
            s.block_out[rows, cols] = (dot(s.att[rows, :], s.wto[:, cols]) + stream).astype(BF16)

        rows = pl.ds(c * CLIP, CLIP)
        pltpu.make_async_copy(
            s.block_out.at[rows, :], s.block_out_out.at[rows, :], s.local.at[20 + c]
        ).start()

        pump(f"out{c}")

    for c in range(2):
        rows = pl.ds(c * CLIP, CLIP)
        exchange_wait(s.recv_d, c, s.sem_d.at[1, c])

        @loop(4)
        def _(r):
            rows = rows_at(c * CLIP + r * 64, 64)
            s.low[rows, :] = s.recv_d[c, ds(r, 8)].astype(F32).reshape(64, D).astype(BF16)

        @loop(2)
        def _(n):
            cols = ds(n, 512)
            s.da[rows, cols] = dot_nt(s.low[rows, :], s.wso[cols, :]).astype(BF16)

        pump(f"att{c}")

        for g in range(2):

            units = [(rows, g * 4 + n) for n in range(4)]
            attention(units, s.qkv, d_att=s.da, d_qkv=s.tqkv)
            pump(f"heads{c}{g}")

        @loop(4)
        def _(n):
            cols = ds(n, 256)
            s.grad[rows, cols] = dot_nt(s.tqkv[rows, :], s.wsq[cols, :])

        pump(f"in{c}")

        @loop(4)
        def _(r):
            rows = rows_at(c * CLIP + r * 64, 64)
            normed, rstd = normalize(s.x[rows, :].astype(F32))
            grad = s.low[rows, :].astype(F32) + norm_back(normed, rstd, s.grad[rows, :])
            s.grad[rows, :] = grad

        pltpu.make_async_copy(s.grad.at[rows, :], s.gin_out.at[rows, :], s.local.at[18 + c]).start()

        pump(f"norm{c}")

    drain(*chunks)
    copies.finish()
    for g in range(4):
        for i in range(3):
            cols = pl.ds(i * D + g * 256, 256)
            pltpu.make_async_copy(
                s.gtm.at[:, cols], s.gtm_out.at[:, cols], s.local.at[6 + g * 3 + i]
            ).wait()
    for c in range(2):
        rows = pl.ds(c * CLIP, CLIP)
        pltpu.make_async_copy(s.grad.at[rows, :], s.gin_out.at[rows, :], s.local.at[18 + c]).wait()
        pltpu.make_async_copy(
            s.block_out.at[rows, :], s.block_out_out.at[rows, :], s.local.at[20 + c]
        ).wait()
        exchange_wait(s.send, c, s.sem_d.at[0, c])


class Scratch:
    def __init__(self, pairs):
        for name, ref in pairs:
            setattr(self, name, ref)


ANY = pl.BlockSpec(memory_space=pl.ANY)


def body(frames_in, sp_qkv, sp_out, tm_qkv, tm_out, cotangent):
    low = lambda *shape: pltpu.VMEM(shape, BF16)
    dma = pltpu.SemaphoreType.DMA
    scratch = dict(
        x=low(T, D), cot=low(T, D), wsq=low(D, 3 * D), wso=low(D, D), wtq=low(D, 3 * D), wto=low(D, D),
        qkv=low(T, 3 * D), att=low(T, D), low=low(T, D), low_t=low(D, T),
        tqkv=low(T, 3 * D), da=low(T, D), dqkv=low(T, 3 * D), bias=pltpu.VMEM((CLIP, CLIP), F32),
        send=low(2, 32, 8, D), recv_s=low(2, 32, 8, D),
        recv_d=low(2, 32, 8, D),
        give=low(4, 2, 256, 768), take=low(4, 2, 256, 768), held=low(4, 2, 256, 768),
        rb=low(4, 3, 2, 64, 768), ra=low(4, 3, 2, 16, 768), rz=low(4, 4, 16, 768),
        total=low(4, 256, 768), rx=low(2, 256, 768), grad=pltpu.VMEM((T, D), F32),
        local=dma((22,)), block_out=low(T, D), gtm=pltpu.VMEM((256, 3 * D), F32), sent=dma((COPIES,)), got=dma((COPIES,)), sem_s=dma((2, 2)), sem_d=dma((2, 2)),
    )
    names = ["x_hbm", "sp_qkv", "sp_out", "tm_qkv", "tm_out", "cot_hbm", "block_out_out", "gin_out", "gtm_out"]
    block_out, grad_in, grad_tm = pl.pallas_call(
        functools.partial(kernel, names + list(scratch)),
        out_shape=[
            jax.ShapeDtypeStruct((T, D), BF16),
            jax.ShapeDtypeStruct((T, D), F32),
            jax.ShapeDtypeStruct((256, 3 * D), F32),
        ],
        in_specs=[ANY] * 6,
        out_specs=[ANY] * 3,
        scratch_shapes=list(scratch.values()),
        compiler_params=pltpu.CompilerParams(
            vmem_limit_bytes=VMEM_LIMIT, collective_id=0, has_side_effects=True
        ),
        name="block",
    )(frames_in.reshape(T, D), sp_qkv, sp_out, tm_qkv, tm_out, cotangent.reshape(T, D))
    return (block_out.reshape(cotangent.shape), grad_in.reshape(frames_in.shape), grad_tm)


COPIES = 200
ACROSS_FIRST = (False, False, True, True)
PLAN = dict(
    group1=(0,), group2=(1,), group3=(2,), grad0=(3,), grad1=(0,), out0=(1,), out1=(0,),
    att0=(2, 1), heads00=(0,), heads01=(1, 3), in0=(2, 0), norm0=(3, 1), att1=(2, 0),
    heads10=(3, 1), heads11=(2,), in1=(3, 2), norm1=(3, 2),
)


def solution(mesh):
    in_specs = (
        P("fsdp", "frame", None, None),
        P("fsdp", None),
        P("fsdp", None),
        P("fsdp", None),
        P("fsdp", None),
        P("fsdp", None, "frame", None),
    )
    out_specs = (P("fsdp", None, "frame", None), P("fsdp", "frame", None, None), P("fsdp", None))
    return jax.shard_map(body, mesh=mesh, in_specs=in_specs, out_specs=out_specs, check_vma=False)
```

```python
import functools

import jax
import jax.numpy as jnp
from jax import lax
from jax.experimental import pallas as pl
from jax.experimental.pallas import tpu as pltpu
from jax.sharding import PartitionSpec as P

MESH = pl.DeviceIdType.MESH
F32 = jnp.float32
BF16 = jnp.bfloat16
EPS = 1e-05
HEADS = 8
HEAD = 128
SCALE = HEAD**-0.5
D = 1024
T = 512
CLIP = 256
VMEM_LIMIT = 60 * 1024 * 1024


def dot(left, right):
    return lax.dot_general(left, right, (((1,), (0,)), ((), ())), preferred_element_type=F32)


def dot_nt(left, right):
    return lax.dot_general(left, right, (((1,), (1,)), ((), ())), preferred_element_type=F32)


def dot_tn(left, right):
    return lax.dot_general(left, right, (((0,), (0,)), ((), ())), preferred_element_type=F32)


def ds(index, size):
    return pl.ds(pl.multiple_of(index * size, size), size)


def loop(count, unroll=1):
    def run(body):
        def step(i, carry):
            body(i)
            return carry

        lax.fori_loop(0, count, step, 0, unroll=unroll)

    return run


def normalize(u):
    mean = jnp.mean(u, axis=-1, keepdims=True)
    cent = u - mean
    rstd = lax.rsqrt(jnp.mean(cent * cent, axis=-1, keepdims=True) + EPS)
    return cent * rstd, rstd


def norm_back(normed, rstd, grad):
    first = jnp.mean(grad, axis=-1, keepdims=True)
    second = jnp.mean(grad * normed, axis=-1, keepdims=True)
    return rstd * (grad - first - normed * second)


def softmax(scores):
    top = jnp.max(scores, axis=-1, keepdims=True)
    expo = jnp.exp(scores - top)
    return expo / jnp.sum(expo, axis=-1, keepdims=True)


def part(i, head):
    return pl.ds(pl.multiple_of((i * HEADS + head) * HEAD, HEAD), HEAD)


def attention(units, qkv, bias=None, att=None, d_att=None, d_qkv=None):
    q, k, v = ([qkv[rows, part(i, head)] for rows, head in units] for i in range(3))
    n = range(len(units))
    scores = [dot_nt(q[i], k[i]) * SCALE for i in n]
    if d_att is not None:
        a = [d_att[rows, part(0, head)] for rows, head in units]
        d_probs = [dot_nt(a[i], v[i]) for i in n]
    if bias is not None:
        scores = [scores[i] + bias[...] for i in n]
    probs = [softmax(scores[i]) for i in n]
    low = [probs[i].astype(BF16) for i in n]
    if att is not None:
        for i, (rows, head) in enumerate(units):
            att[rows, part(0, head)] = dot(low[i], v[i]).astype(BF16)
    if d_att is None:
        return
    for i, (rows, head) in enumerate(units):
        d_qkv[rows, part(2, head)] = dot_tn(low[i], a[i]).astype(BF16)
    prod = [d_probs[i] * probs[i] for i in n]
    d_s = [
        ((prod[i] - probs[i] * jnp.sum(prod[i], axis=-1, keepdims=True)) * SCALE).astype(BF16)
        for i in n
    ]
    for i, (rows, head) in enumerate(units):
        d_qkv[rows, part(0, head)] = dot(d_s[i], k[i]).astype(BF16)
    for i, (rows, head) in enumerate(units):
        d_qkv[rows, part(1, head)] = dot_tn(d_s[i], q[i]).astype(BF16)


def rows_at(index, size):
    return pl.ds(pl.multiple_of(index, size), size)


class Place:
    def __init__(self):
        frame, fsdp = lax.axis_index("frame"), lax.axis_index("fsdp")
        self.lo, x, y = lax.div(frame, 16), lax.rem(lax.div(frame, 4), 4), lax.rem(frame, 4)
        self.hi, self.core = lax.div(fsdp, 2), lax.rem(fsdp, 2)
        self.x, self.y = x, y
        self.a = x + self.core * (y - x)
        self.b = y + self.core * (x - y)
        self.ap, self.am = lax.rem(self.a + 1, 4), lax.rem(self.a + 3, 4)
        self.bp, self.bm = lax.rem(self.b + 1, 4), lax.rem(self.b + 3, 4)
        self.a2, self.b2 = lax.rem(self.a + 2, 4), lax.rem(self.b + 2, 4)
        self.fsdp, self.frame = fsdp, frame
        self.far = (frame, (1 - self.hi) * 2 + self.core)
        self.sibling = (frame, self.hi * 2 + 1 - self.core)
        self.cross = ((1 - self.lo) * 16 + x * 4 + y, (1 - self.hi) * 2 + self.core)
        self.twin = ((1 - self.lo) * 16 + x * 4 + y, fsdp)
        self.a_next, self.a_prev = self.at(self.ap, self.b), self.at(self.am, self.b)
        self.b_next, self.b_prev = self.at(self.a, self.bp), self.at(self.a, self.bm)

    def at(self, a, b):
        x = a + self.core * (b - a)
        y = b + self.core * (a - b)
        return (self.lo * 16 + x * 4 + y, self.fsdp)


class Copies:
    def __init__(self, send, recv):
        self.send, self.recv, self.count, self.started = send, recv, 0, []

    def start(self, src, dst, device):
        i = self.count
        self.count += 1
        copy = pltpu.make_async_remote_copy(
            src_ref=src, dst_ref=dst, send_sem=self.send.at[i], recv_sem=self.recv.at[i],
            device_id=device, device_id_type=MESH,
        )
        copy.start()
        self.started.append(copy)
        return copy

    def finish(self):
        for copy in self.started:
            copy.wait_send()


def exchange_start(here, send, recv, clip, sems):
    recv[clip, here.frame] = send[clip, here.frame]

    @loop(31)
    def _(d):
        peer = lax.rem(here.frame + 1 + d, 32)
        pltpu.make_async_remote_copy(
            src_ref=send.at[clip, peer], dst_ref=recv.at[clip, here.frame],
            send_sem=sems.at[0, clip], recv_sem=sems.at[1, clip],
            device_id=(peer, here.fsdp), device_id_type=MESH,
        ).start()


def exchange_wait(buffer, clip, sem):
    block = buffer.at[clip, pl.ds(0, 31)]
    pltpu.make_async_copy(block, block, sem).wait()


def gather(copies, here, shard, out):
    own = here.fsdp * 256
    base = ((1 - here.hi) * 2 + here.core) * 256
    piece = (here.b * 4 + here.a) * 16
    row = (here.ap, here.am, here.a2)
    src, dst = shard.at[rows_at(piece, 16), :], out.at[rows_at(own + piece, 16), :]
    cross = copies.start(src, dst, here.cross)
    yield
    cross.wait_recv()
    block = out.at[rows_at(base + piece, 16), :]
    sent = [copies.start(block, block, here.at(a, here.b)) for a in row]
    yield
    for copy in sent:
        copy.wait_recv()
    block = out.at[rows_at(base + here.b * 64, 64), :]
    sent = [copies.start(block, block, here.at(here.a, b)) for b in (here.bp, here.bm, here.b2)]
    over = [copies.start(block, block, here.sibling)]
    yield
    for copy in sent:
        copy.wait_recv()
    for b in (here.bp, here.bm, here.b2):
        block = out.at[rows_at(base + b * 64, 64), :]
        over.append(copies.start(block, block, here.sibling))
    yield
    for copy in over:
        copy.wait_recv()


def gather_whole(copies, here, shard, out):
    own = rows_at(here.fsdp * 256, 256)
    cross = copies.start(shard, out.at[own, :], here.cross)
    yield
    cross.wait_recv()
    block = out.at[rows_at(((1 - here.hi) * 2 + here.core) * 256, 256), :]
    over = copies.start(block, block, here.sibling)
    yield
    over.wait_recv()


def gather_across(copies, here, shard, out):
    half = rows_at(here.fsdp * 256 + (1 - here.lo) * 128, 128)
    cross = copies.start(shard.at[rows_at((1 - here.lo) * 128, 128), :], out.at[half, :], here.cross)
    yield
    cross.wait_recv()
    base = ((1 - here.hi) * 2 + here.core) * 256
    block = out.at[rows_at(base + here.lo * 128, 128), :]
    twin = copies.start(block, block, here.twin)
    over = [copies.start(block, block, here.sibling)]
    yield
    twin.wait_recv()
    block = out.at[rows_at(base + (1 - here.lo) * 128, 128), :]
    over.append(copies.start(block, block, here.sibling))
    yield
    for copy in over:
        copy.wait_recv()


def reduce_chunk(copies, here, s, g, across_first):
    give, take, held, rb, ra, rz, total = (
        r.at[g] for r in (s.give, s.take, s.held, s.rb, s.ra, s.rz, s.total)
    )
    for h in range(2):
        for i in range(3):
            cols = pl.ds(i * D + g * 256, 256)
            to = pl.ds(i * 256, 256)
            for core, ref in ((1 - here.core, give), (here.core, held)):
                left = s.low_t[rows_at((h * 2 + core) * 256, 256), :]
                ref[h, :, to] = dot(left, s.dqkv[:, cols]).astype(BF16)
    over = copies.start(give, take, here.sibling)
    yield
    over.wait_recv()
    for h in range(2):
        held[h] = (held[h].astype(F32) + take[h].astype(F32)).astype(BF16)
    shards, count = slice(None), 2
    if across_first:
        rx = s.rx.at[sum(ACROSS_FIRST[:g])]
        cross = copies.start(held.at[1 - here.hi], rx, here.cross)
        yield
        cross.wait_recv()
        held[here.hi] = (held[here.hi].astype(F32) + rx[...].astype(F32)).astype(BF16)
        shards, count = pl.ds(here.hi, 1), 1

    def scatter(size, offset, at, others, device, dst):
        sent = []
        for i, other in enumerate(others):
            block = held.at[shards, rows_at(offset + other * size, size), :]
            sent.append(copies.start(block, dst.at[i, pl.ds(0, count)], device(other)))
        yield
        for copy in sent:
            copy.wait_recv()
        rows = rows_at(offset + at * size, size)
        sum_ = held[shards, rows, :].astype(F32)
        for i in range(3):
            sum_ = sum_ + dst[i, :count].astype(F32)
        held[shards, rows, :] = sum_.astype(BF16)

    base = here.b * 64
    yield from scatter(
        64, 0, here.b, (here.bp, here.b2, here.bm), lambda b: here.at(here.a, b), rb
    )
    yield from scatter(
        16, base, here.a, (here.ap, here.a2, here.am), lambda a: here.at(a, here.b), ra
    )

    mine = rows_at(base + here.a * 16, 16)
    own = held.at[here.hi, mine, :]
    if across_first:
        sent = [copies.start(own, rz.at[0], here.twin)]
    else:
        slot = here.lo * 2 + here.hi
        rz[slot] = own[...]
        other = held.at[1 - here.hi, mine, :]
        sent = [copies.start(own, rz.at[slot], here.twin)]
        sent += [copies.start(other, rz.at[slot], to) for to in (here.cross, here.far)]
    yield
    for copy in sent:
        copy.wait_recv()
    sum_ = rz[0].astype(F32)
    if across_first:
        sum_ = sum_ + own[...].astype(F32)
    else:
        for i in range(1, 4):
            sum_ = sum_ + rz[i].astype(F32)
    total[mine, :] = sum_.astype(BF16)

    block = total.at[mine, :]
    sent = [copies.start(block, block, here.at(a, here.b)) for a in (here.ap, here.am, here.a2)]
    yield
    for copy in sent:
        copy.wait_recv()
    block = total.at[rows_at(base, 64), :]
    sent = [copies.start(block, block, here.at(here.a, b)) for b in (here.bp, here.bm, here.b2)]
    yield
    for copy in sent:
        copy.wait_recv()
    for i in range(3):
        cols = pl.ds(i * D + g * 256, 256)
        s.gtm[:, cols] = total[:, pl.ds(i * 256, 256)].astype(F32)
        pltpu.make_async_copy(s.gtm.at[:, cols], s.gtm_out.at[:, cols], s.local.at[6 + g * 3 + i]).start()


def kernel(names, *refs):
    s = Scratch(zip(names, refs))
    here = Place()
    loads = {}
    for i, (src, dst) in enumerate((
        (s.x_hbm, s.x),
        (s.sp_qkv, s.wsq.at[rows_at(here.fsdp * 256, 256), :]),
        (s.sp_out, s.wso.at[rows_at(here.fsdp * 256, 256), :]),
        (s.tm_qkv, s.wtq.at[rows_at(here.fsdp * 256, 256), :]),
        (s.tm_out, s.wto.at[rows_at(here.fsdp * 256, 256), :]),
        (s.cot_hbm, s.cot),
    )):
        loads[i] = pltpu.make_async_copy(src, dst, s.local.at[i])
        loads[i].start()

    barrier = pltpu.get_barrier_semaphore()

    @loop(31)
    def _(d):
        peer = lax.rem(here.frame + 1 + d, 32)
        pl.semaphore_signal(barrier, inc=1, device_id=(peer, here.fsdp), device_id_type=MESH)

    for device in (here.sibling, here.cross, here.far):
        pl.semaphore_signal(barrier, inc=1, device_id=device, device_id_type=MESH)
    copies = Copies(s.sent, s.got)

    def drain(*many):
        for steps in many:
            for _ in steps:
                pass

    def step(*many):
        for steps in many:
            next(steps)

    thirds = [pl.ds(i * D, D) for i in range(3)]
    halves = [[pl.ds(i * D + n * 512, 512) for i in range(3)] for n in range(2)]
    sp = [
        [gather(copies, here, s.sp_qkv.at[:, c], s.wsq.at[:, c]) for c in halves[n]]
        for n in range(2)
    ]
    sp_out = gather_across(copies, here, s.sp_out, s.wso)
    tm = [
        how(copies, here, s.tm_qkv.at[:, c], s.wtq.at[:, c])
        for how, c in zip((gather, gather_across, gather), thirds)
    ]
    tm_out = gather_whole(copies, here, s.tm_out, s.wto)

    loads[0].wait()

    @loop(8)
    def _(r):
        rows = ds(r, 64)
        s.low[rows, :] = normalize(s.x[rows, :].astype(F32))[0].astype(BF16)

    pl.semaphore_wait(barrier, 34)
    step(*sp[0], *sp[1])

    def over(shard, out):
        return copies.start(shard, out.at[rows_at(here.fsdp * 256, 256), :], here.sibling)

    mine = [over(s.sp_qkv, s.wsq), over(s.sp_out, s.wso)]
    step(sp_out, *tm)

    row = lax.broadcasted_iota(jnp.int32, (CLIP, CLIP), 0)
    col = lax.broadcasted_iota(jnp.int32, (CLIP, CLIP), 1)
    allowed = (col <= row) & (((row - col) & 7) == 0)
    s.bias[...] = jnp.where(allowed, 0.0, -1e30)

    step(*sp[0], *sp[1])
    step(*sp[0])
    step(*sp[1])
    step(sp_out, tm_out)
    step(tm[0], tm[2])
    step(*sp[0])
    mine[0].wait_recv()
    loads[1].wait()

    def project(n):
        drain(*sp[n])
        for i in range(3):
            cols = halves[n][i]
            s.qkv[:, cols] = dot(s.low[...], s.wsq[:, cols]).astype(BF16)

    def attend(n, c):
        rows = pl.ds(c * CLIP, CLIP)
        attention([(rows, n * 4 + j) for j in range(4)], s.qkv, att=s.att)

    project(0)
    step(*sp[1])
    step(tm[0], tm[2], tm[1])
    attend(0, 0)
    attend(0, 1)
    project(1)
    step(sp_out)
    mine += [over(s.tm_qkv, s.wtq), over(s.tm_out, s.wto)]
    for c in range(2):
        attend(1, c)
        if c == 0:
            drain(sp_out)
            mine[1].wait_recv()
            loads[2].wait()
        rows = pl.ds(c * CLIP, CLIP)

        @loop(4)
        def _(n):
            cols = ds(n, 256)
            out = dot(s.att[rows, :], s.wso[:, cols]) + s.x[rows, cols].astype(F32)
            s.send[c, :, :, cols] = out.reshape(32, 8, 256).astype(BF16)

        exchange_start(here, s.send, s.recv_s, c, s.sem_s)

    step(tm_out)
    step(*tm)
    drain(*tm, tm_out)
    mine[2].wait_recv()
    mine[3].wait_recv()
    for i in (3, 4, 5):
        loads[i].wait()

    @loop(2)
    def _(n):
        cols = ds(n, 512)
        s.da[:, cols] = dot_nt(s.cot[...], s.wto[cols, :]).astype(BF16)

    for c in range(2):
        exchange_wait(s.recv_s, c, s.sem_s.at[1, c])

        @loop(4)
        def _(r):
            rows = rows_at(c * CLIP + r * 64, 64)
            u = s.recv_s[c, ds(r, 8)].astype(F32).reshape(64, D)
            s.low[rows, :] = normalize(u)[0].astype(BF16)

        rows = pl.ds(c * CLIP, CLIP)
        s.low_t[:, rows] = s.low[rows, :].T
        if c == 0:

            @loop(6)
            def _(n):
                cols = ds(n, 512)
                s.tqkv[:CLIP, cols] = dot(s.low[:CLIP, :], s.wtq[:, cols]).astype(BF16)

    def pump(point):
        for g in PLAN.get(point, ()):
            next(chunks[g], None)

    chunks = [reduce_chunk(copies, here, s, g, ACROSS_FIRST[g]) for g in range(4)]
    for g in range(4):

        for i in range(3):
            cols = pl.ds(i * D + g * 256, 256)
            s.tqkv[CLIP:, cols] = dot(s.low[CLIP:, :], s.wtq[:, cols]).astype(BF16)

        units = [(pl.ds(c * CLIP, CLIP), g * 2 + n) for n in range(2) for c in range(2)]
        attention(units, s.tqkv, s.bias, s.att, s.da, s.dqkv)
        step(chunks[g])
        pump(f"group{g}")

    for c in range(2):
        rows = pl.ds(c * CLIP, CLIP)

        @loop(4)
        def _(n):
            cols = ds(n, 256)
            s.grad[rows, cols] = dot_nt(s.dqkv[rows, :], s.wtq[cols, :])

        pump(f"grad{c}")
        exchange_wait(s.send, c, s.sem_s.at[0, c])

        @loop(4)
        def _(r):
            rows = rows_at(c * CLIP + r * 64, 64)
            normed, rstd = normalize(s.recv_s[c, ds(r, 8)].astype(F32).reshape(64, D))
            grad = s.cot[rows, :].astype(F32) + norm_back(normed, rstd, s.grad[rows, :])
            s.send[c, ds(r, 8)] = grad.reshape(8, 8, D).astype(BF16)

        exchange_start(here, s.send, s.recv_d, c, s.sem_d)

    for c in range(2):

        @loop(2)
        def _(n):
            cols = ds(n, 512)
            rows = pl.ds(c * CLIP, CLIP)
            stream = s.recv_s[c, :, :, cols].astype(F32).reshape(CLIP, 512)
            s.block_out[rows, cols] = (dot(s.att[rows, :], s.wto[:, cols]) + stream).astype(BF16)

        rows = pl.ds(c * CLIP, CLIP)
        pltpu.make_async_copy(
            s.block_out.at[rows, :], s.block_out_out.at[rows, :], s.local.at[20 + c]
        ).start()

        pump(f"out{c}")

    for c in range(2):
        rows = pl.ds(c * CLIP, CLIP)
        exchange_wait(s.recv_d, c, s.sem_d.at[1, c])

        @loop(4)
        def _(r):
            rows = rows_at(c * CLIP + r * 64, 64)
            s.low[rows, :] = s.recv_d[c, ds(r, 8)].astype(F32).reshape(64, D).astype(BF16)

        @loop(2)
        def _(n):
            cols = ds(n, 512)
            s.da[rows, cols] = dot_nt(s.low[rows, :], s.wso[cols, :]).astype(BF16)

        pump(f"att{c}")

        for g in range(2):

            units = [(rows, g * 4 + n) for n in range(4)]
            attention(units, s.qkv, d_att=s.da, d_qkv=s.tqkv)
            pump(f"heads{c}{g}")

        @loop(4)
        def _(n):
            cols = ds(n, 256)
            s.grad[rows, cols] = dot_nt(s.tqkv[rows, :], s.wsq[cols, :])

        pump(f"in{c}")

        @loop(4)
        def _(r):
            rows = rows_at(c * CLIP + r * 64, 64)
            normed, rstd = normalize(s.x[rows, :].astype(F32))
            grad = s.low[rows, :].astype(F32) + norm_back(normed, rstd, s.grad[rows, :])
            s.grad[rows, :] = grad

        pltpu.make_async_copy(s.grad.at[rows, :], s.gin_out.at[rows, :], s.local.at[18 + c]).start()

        pump(f"norm{c}")

    for _ in range(8):
        for steps in chunks:
            next(steps, None)
    copies.finish()
    for g in range(4):
        for i in range(3):
            cols = pl.ds(i * D + g * 256, 256)
            pltpu.make_async_copy(
                s.gtm.at[:, cols], s.gtm_out.at[:, cols], s.local.at[6 + g * 3 + i]
            ).wait()
    for c in range(2):
        rows = pl.ds(c * CLIP, CLIP)
        pltpu.make_async_copy(s.grad.at[rows, :], s.gin_out.at[rows, :], s.local.at[18 + c]).wait()
        pltpu.make_async_copy(
            s.block_out.at[rows, :], s.block_out_out.at[rows, :], s.local.at[20 + c]
        ).wait()
        exchange_wait(s.send, c, s.sem_d.at[0, c])


class Scratch:
    def __init__(self, pairs):
        for name, ref in pairs:
            setattr(self, name, ref)


ANY = pl.BlockSpec(memory_space=pl.ANY)


def body(frames_in, sp_qkv, sp_out, tm_qkv, tm_out, cotangent):
    low = lambda *shape: pltpu.VMEM(shape, BF16)
    dma = pltpu.SemaphoreType.DMA
    scratch = dict(
        x=low(T, D), cot=low(T, D), wsq=low(D, 3 * D), wso=low(D, D), wtq=low(D, 3 * D), wto=low(D, D),
        qkv=low(T, 3 * D), att=low(T, D), low=low(T, D), low_t=low(D, T),
        tqkv=low(T, 3 * D), da=low(T, D), dqkv=low(T, 3 * D), bias=pltpu.VMEM((CLIP, CLIP), F32),
        send=low(2, 32, 8, D), recv_s=low(2, 32, 8, D),
        recv_d=low(2, 32, 8, D),
        give=low(4, 2, 256, 768), take=low(4, 2, 256, 768), held=low(4, 2, 256, 768),
        rb=low(4, 3, 2, 64, 768), ra=low(4, 3, 2, 16, 768), rz=low(4, 4, 16, 768),
        total=low(4, 256, 768), rx=low(2, 256, 768), grad=pltpu.VMEM((T, D), F32),
        local=dma((22,)), block_out=low(T, D), gtm=pltpu.VMEM((256, 3 * D), F32), sent=dma((COPIES,)), got=dma((COPIES,)), sem_s=dma((2, 2)), sem_d=dma((2, 2)),
    )
    names = ["x_hbm", "sp_qkv", "sp_out", "tm_qkv", "tm_out", "cot_hbm", "block_out_out", "gin_out", "gtm_out"]
    block_out, grad_in, grad_tm = pl.pallas_call(
        functools.partial(kernel, names + list(scratch)),
        out_shape=[
            jax.ShapeDtypeStruct((T, D), BF16),
            jax.ShapeDtypeStruct((T, D), F32),
            jax.ShapeDtypeStruct((256, 3 * D), F32),
        ],
        in_specs=[ANY] * 6,
        out_specs=[ANY] * 3,
        scratch_shapes=list(scratch.values()),
        compiler_params=pltpu.CompilerParams(
            vmem_limit_bytes=VMEM_LIMIT, collective_id=0, has_side_effects=True
        ),
        name="block",
    )(frames_in.reshape(T, D), sp_qkv, sp_out, tm_qkv, tm_out, cotangent.reshape(T, D))
    return (block_out.reshape(cotangent.shape), grad_in.reshape(frames_in.shape), grad_tm)


COPIES = 200
ACROSS_FIRST = (False, False, True, True)
PLAN = dict(
    group1=(0,), group2=(1,), group3=(2,), grad0=(3,), out1=(0, 1), heads00=(0, 1, 2),
    heads01=(0, 1, 3), in0=(2, 0, 1), att1=(3, 2, 0, 1), heads10=(3, 2), heads11=(3, 2),
    in1=(3, 2), norm1=(3, 2),
)


def solution(mesh):
    in_specs = (
        P("fsdp", "frame", None, None),
        P("fsdp", None),
        P("fsdp", None),
        P("fsdp", None),
        P("fsdp", None),
        P("fsdp", None, "frame", None),
    )
    out_specs = (P("fsdp", None, "frame", None), P("fsdp", "frame", None, None), P("fsdp", None))
    return jax.shard_map(body, mesh=mesh, in_specs=in_specs, out_specs=out_specs, check_vma=False)
```
